512 devices in a mesh: mem: 64 (over z, y_lo, core), tile: 8 (over y_hi, x).
Axes of the slice: x: 4, y: 4 (y_hi: 2, y_lo: 2; y = y_hi * 2 + y_lo), z: 16, core: 2. Of those that a mesh axis runs over, the one named last changes fastest.
Arguments:
- background: float32 [2, 256, 1024], P(None, 'tile'), may hold values from -6 to 6
- anomalies: float32 [64, 2, 256, 1024], P('mem', None, 'tile'), may hold values from -6 to 6
- courant_lon: float32 [2, 256, 1024], P(None, 'tile'), may hold values from -0.12 to 0.12
- courant_lat: float32 [2, 256, 1024], P(None, 'tile'), may hold values from -0.85 to 0.85
- obs_value: float32 [32768], P('tile'), may hold values from -12 to 12
- obs_weight: float32 [32768], P('tile'), may hold values from 0.015 to 0.15
- obs_column: int32 [32768], P('tile'), may hold values from 0 to 32767
- obs_level: int32 [32768], P('tile'), may hold values from 0 to 1
Outputs:
- increment: float32 [2, 256, 1024], P(None, 'tile')
The draws below stay inside these ranges and needn't reach their ends.
All inputs are finite; a program needn't handle non-finite values.
Results may differ from the reference program's by a relative error of at most 0.00026.
Values sent between devices are 32-bit elements; how exact they have to be, the bound alone decides.
No kernel may reach another device: no remote copies, remote signals or barrier semaphores. Data moves between devices by JAX's collectives and lax.ppermute only.
A program may use at most 64 MiB of HBM per device.

```python
import math
import jax
import jax.numpy as jnp
from jax import lax

LEV = 2
CY = 32
NX = 1024
OBS_TILE = 4096
NSTEP = 8
ITERS = 2
MEMBERS = 64
NY = 256
NOBS = 32768


def set_ends(result, own_key, low, largest):
    longest = result.shape.index(max(result.shape))
    spots = []
    for shift in (0, 1):
        where = [jax.random.randint(jax.random.fold_in(own_key, axis), (), 0, length) for axis, length in enumerate(result.shape)]
        where[longest] = (where[longest] + shift) % result.shape[longest]
        spots.append(tuple(where))
    return result.at[spots[0]].set(low).at[spots[1]].set(largest)


def block_scale(rng, dims, pieces, low, top_value):
    gain, own = 1.0, jax.random.fold_in(rng, 6)
    for dim, shards_of in pieces:
        steps = jnp.exp(jax.random.uniform(jax.random.fold_in(own, dim), (shards_of,), jnp.float32, low / len(pieces), top_value / len(pieces)))
        gain = gain * jnp.repeat(steps, dims[dim] // shards_of).reshape([-1 if axis == dim else 1 for axis in range(len(dims))])
    return gain


def centred(rng, dims, deviation, reach, shards=(), held_as=jnp.bfloat16):
    level = block_scale(rng, dims, shards, -0.22, 0.18) if shards else 1.0
    drawn = jax.random.normal(rng, dims, jnp.float32) * deviation * level
    return jnp.minimum(jnp.maximum(drawn, -reach), reach).astype(held_as)


def setup_inputs(seed: int = 0) -> dict:
    streams_of = jax.random.split(jax.random.key(seed), 9)
    return {
        "background": centred(streams_of[0], (LEV, NY, NX), 1.0, 6.0, ((1, 8),), jnp.float32),
        "anomalies": centred(streams_of[1], (MEMBERS, LEV, NY, NX), 1.0, 6.0, ((0, 64), (2, 8)), jnp.float32),
        "courant_lon": jnp.clip(jax.random.uniform(streams_of[2], (LEV, NY, NX), jnp.float32, -0.12, 0.12) * block_scale(streams_of[2], (LEV, NY, NX), ((1, 8),), -0.4, 0.0), -0.12, 0.12),
        "courant_lat": jnp.clip(jax.random.uniform(streams_of[3], (LEV, NY, NX), jnp.float32, -0.85, 0.85) * block_scale(streams_of[3], (LEV, NY, NX), ((1, 8),), -0.4, 0.0), -0.85, 0.85),
        "obs_value": centred(streams_of[4], (NOBS,), 3.0, 12.0, ((0, 8),), jnp.float32),
        "obs_weight": jnp.clip(jnp.exp(math.log(0.15) - 2.3025852 * jax.random.uniform(streams_of[5], (NOBS,), jnp.float32) ** block_scale(streams_of[5], (NOBS,), ((0, 8),), -0.2, 0.2)), 0.015, 0.15),
        "obs_column": set_ends(jax.random.randint(streams_of[6], (NOBS,), 0, CY * NX), jax.random.fold_in(streams_of[6], 1), 0, (CY * NX) - 1).astype(jnp.int32),
        "obs_level": set_ends(jax.random.randint(streams_of[7], (NOBS,), 0, LEV), jax.random.fold_in(streams_of[7], 1), 0, LEV - 1).astype(jnp.int32),
    }


bundle_scale = 0.5
quad_coef = 0.25
speed_base = 0.85
speed_gain = 0.15

def advance(field, courant_lon, courant_lat):
    padded = jnp.pad(field, ((0, 0), (1, 1), (0, 0)))
    south = padded[:, :-2, :]
    north = padded[:, 2:, :]
    west = jnp.roll(field, 1, axis=2)
    east = jnp.roll(field, -1, axis=2)
    factor = speed_base + speed_gain * jnp.tanh(field)
    along_lon = factor * courant_lon
    along_lat = factor * courant_lat
    zonal_flux = jnp.maximum(along_lon, 0.0) * (field - west) + jnp.minimum(along_lon, 0.0) * (east - field)
    merid_flux = jnp.maximum(along_lat, 0.0) * (field - south) + jnp.minimum(along_lat, 0.0) * (north - field)
    return field - zonal_flux - merid_flux

def propagate(field, courant_lon, courant_lat):
    for sweep_index in range(NSTEP):
        field = advance(field, courant_lon, courant_lat)
    return field

def observe(state, obs_column, obs_level):
    number = obs_column.shape[0]
    tile_of = (jnp.arange(number, dtype=jnp.int32) // OBS_TILE).astype(jnp.int32)
    row_index = (tile_of * CY + obs_column // NX).astype(jnp.int32)
    col_index = (obs_column % NX).astype(jnp.int32)
    sampled = state[obs_level, row_index, col_index]
    return sampled + quad_coef * sampled * sampled

def normal_terms(observed, obs_value, obs_weight):
    center = jnp.mean(observed, axis=0)
    spread = (observed - center[None, :]) / bundle_scale * obs_weight[None, :]
    misfit = (obs_value - center) * obs_weight
    gram_mat = jnp.dot(spread, spread.T, precision=lax.Precision.HIGHEST)
    project = jnp.dot(spread, misfit, precision=lax.Precision.HIGHEST)
    return (gram_mat, project)

def newton_update(weights, gram_mat, project):
    members = weights.shape[0]
    hessian = gram_mat + (members - 1) * jnp.eye(members, dtype=jnp.float32)
    gradient = (members - 1) * weights - project
    chol_low = jnp.linalg.cholesky(hessian)
    forward_sol = lax.linalg.triangular_solve(chol_low, gradient[:, None], left_side=True, lower=True)
    solved = lax.linalg.triangular_solve(chol_low, forward_sol, left_side=True, lower=True, transpose_a=True)
    return weights - solved[:, 0]

def reference(background, anomalies, courant_lon, courant_lat, obs_value, obs_weight, obs_column, obs_level):
    members = anomalies.shape[0]
    weights = jnp.zeros((members,), jnp.float32)
    for iteration in range(ITERS):
        mixed = jnp.einsum('m,mlyx->lyx', weights, anomalies, precision=lax.Precision.HIGHEST)

        def member(single):
            state = background + mixed + bundle_scale * single
            return observe(propagate(state, courant_lon, courant_lat), obs_column, obs_level)
        observed = lax.map(member, anomalies)
        gram_mat, project = normal_terms(observed, obs_value, obs_weight)
        weights = newton_update(weights, gram_mat, project)
    return jnp.einsum('m,mlyx->lyx', weights, anomalies, precision=lax.Precision.HIGHEST)
```

```python
import functools

import jax
import jax.numpy as jnp
from jax import lax
from jax.experimental import pallas as pl
from jax.experimental.pallas import tpu as pltpu
from jax.sharding import Mesh, PartitionSpec as P

NSTEP = 8
MEMBERS = 64
PAIRS = 32
LEV = 2
CY = 32
NX = 1024
CHUNK = 16
HALO = 8
ROWS = CY + 2 * HALO
LANES = 128
HIGHEST = lax.Precision.HIGHEST

MEM = ("z", "yl", "core")
TILE = ("yh", "x")
PLANE = ("yl", "core", "yh", "x")
VMEM = pl.BlockSpec(memory_space=pltpu.VMEM)
SMEM = pl.BlockSpec(memory_space=pltpu.SMEM)


def lane_of(shape):
    return lax.broadcasted_iota(jnp.int32, shape, len(shape) - 1)


def call(body, out, scratch=(), in_specs=None, vmem=40 << 20):
    return pl.pallas_call(
        body,
        out_shape=out,
        in_specs=in_specs,
        out_specs=jax.tree.map(lambda _: VMEM, out),
        scratch_shapes=list(scratch),
        compiler_params=pltpu.CompilerParams(vmem_limit_bytes=vmem),
    )


def f32(*shape):
    return jax.ShapeDtypeStruct(shape, jnp.float32)


def pack_body(chunk_ref, own_ref, bg_ref, lon_ref, lat_ref, pieces_ref, fields_ref):
    lane = lane_of((16, LANES))
    shifted = []
    for group in range(4):
        half, lev = divmod(group, 2)
        rolled = [
            pltpu.roll(
                own_ref[lev, 16 * half : 16 * half + 16, LANES * b : LANES * b + LANES],
                HALO,
                axis=1,
            )
            for b in range(8)
        ]
        shifted.append([jnp.where(lane < HALO, rolled[b - 1], rolled[b]) for b in range(8)])
    for b in range(8):
        for k in range(8):
            out = None
            for group in range(4):
                amount = (32 * group - CHUNK * k) % LANES
                source = shifted[group][b]
                if k == 7:
                    source = jnp.where(lane < CHUNK, shifted[group][(b + 1) % 8], source)
                moved = pltpu.roll(source, amount, axis=1) if amount else source
                out = moved if out is None else jnp.where(lane >= 32 * group, moved, out)
            pieces_ref[8 * b + k] = out
    chunk = chunk_ref[0]
    b, k = chunk // 8, chunk % 8
    wide = lane_of((CY, LANES))

    def block(ref, lev, index):
        return ref[lev, :, pl.ds(pl.multiple_of(index * LANES, LANES), LANES)]

    for index, ref in enumerate((bg_ref, lon_ref, lat_ref)):
        out = None
        for lev in range(LEV):
            mid = block(ref, lev, b)
            low = block(ref, lev, (b + 7) % 8)
            high = block(ref, lev, (b + 1) % 8)
            mid = jnp.where((wide >= LANES - HALO) & (k == 0), low, mid)
            mid = jnp.where((wide < HALO) & (k == 7), high, mid)
            moved = pltpu.roll(mid, (32 * lev + HALO - CHUNK * k + LANES) % LANES, axis=1)
            out = moved if out is None else jnp.where(wide >= 32, moved, out)
        out = jnp.where(wide < 64, out, pltpu.roll(out, 64, axis=1))
        fields_ref[index] = out


def pair_body(x_ref, fields_ref, mid_ref, low_ref, high_ref):
    lane = lane_of((16, LANES))
    for p in range(PAIRS):
        first, second = x_ref[p], x_ref[p + PAIRS]
        upper = jnp.where(lane < 64, first, pltpu.roll(second, 64, axis=1))
        lower = jnp.where(lane < 64, pltpu.roll(first, 64, axis=1), second)
        mid_ref[p, 0:16] = upper
        mid_ref[p, 16:32] = lower
        low_ref[p] = upper[0:HALO]
        high_ref[p] = lower[HALO:16]
    for index in range(3):
        low_ref[PAIRS + index] = fields_ref[index, 0:HALO]
        high_ref[PAIRS + index] = fields_ref[index, CY - HALO : CY]


def cells_body(chunk_ref, value_ref, weight_ref, column_ref, level_ref, out_ref):
    chunk = chunk_ref[0]
    column = column_ref[...]
    row = column // NX
    offset = column % NX - CHUNK * chunk
    inside = (offset >= 0) & (offset < CHUNK)
    lane = jnp.where(inside, level_ref[...] * 32 + HALO + offset, -1)
    square = weight_ref[...] * weight_ref[...]
    nobs = column.shape[1]
    at_row = lax.broadcasted_iota(jnp.int32, (CY, nobs), 0) == row
    at_lane = (lax.broadcasted_iota(jnp.int32, (LANES, nobs), 0) == lane).astype(jnp.bfloat16)
    parts = []
    for value in (square, square * value_ref[...]):
        left = jnp.where(at_row, value, 0.0)
        for _ in range(3):
            part = left.astype(jnp.bfloat16)
            parts.append(part)
            left = left - part.astype(jnp.float32)
    sums = lax.dot_general(
        jnp.concatenate(parts, axis=0),
        at_lane,
        (((1,), (1,)), ((), ())),
        preferred_element_type=jnp.float32,
    )
    for index in range(2):
        base = 3 * CY * index
        total = sums[base : base + CY] + sums[base + CY : base + 2 * CY]
        total = total + sums[base + 2 * CY : base + 3 * CY]
        out_ref[index] = total


def transport(base, anoms_ref, coefs, count, first):
    state = base + 0.5 * anoms_ref[pl.ds(first, count)]
    west_c, east_c, south_c, north_c, own_c = coefs
    for _ in range(NSTEP):
        west = pltpu.roll(state, 1, axis=2)
        east = pltpu.roll(state, LANES - 1, axis=2)
        south = pltpu.roll(state, 1, axis=1)
        north = pltpu.roll(state, ROWS - 1, axis=1)
        speed = 0.85 + 0.15 * jnp.tanh(state)
        change = west_c[...] * west + east_c[...] * east
        change = change + (south_c[...] * south + north_c[...] * north)
        state = state + speed * (change - own_c[...] * state)
    return state


def observe_and_gram(base, anoms_ref, coefs, cells_ref, gram_ref, obs_ref, dev_ref, left_ref, right_ref):
    group = 4

    def one(index, total):
        first = index * group
        state = transport(base, anoms_ref, coefs, group, first)[:, HALO : HALO + CY]
        seen = state + 0.25 * state * state
        obs_ref[pl.ds(first, group)] = seen
        return total + jnp.sum(seen, axis=0)

    total = lax.fori_loop(0, PAIRS // group, one, jnp.zeros((CY, LANES), jnp.float32))
    center = (total + pltpu.roll(total, 64, axis=1)) * (1.0 / MEMBERS)
    lane = lane_of((16, LANES))
    for p in range(PAIRS):
        dev = obs_ref[p] - center
        upper, lower = dev[0:16], dev[16:32]
        dev_ref[16 * p : 16 * p + 16] = jnp.where(lane < 64, upper, pltpu.roll(lower, 64, axis=1))
        at = 16 * (p + PAIRS)
        dev_ref[at : at + 16] = jnp.where(lane < 64, pltpu.roll(upper, 64, axis=1), lower)
    weight, weighted = cells_ref[0], cells_ref[1]
    aim = 2.0 * (weighted - weight * center)
    aim = jnp.where(lane < 64, aim[0:16], pltpu.roll(aim[16:32], 64, axis=1))
    weight = 4.0 * weight
    weight = jnp.where(lane < 64, weight[0:16], pltpu.roll(weight[16:32], 64, axis=1))
    right_ref[MEMBERS:LANES, :] = jnp.zeros((LANES - MEMBERS, 16 * LANES), jnp.float32)
    for r in range(16):
        rows = dev_ref[pl.ds(r, MEMBERS, stride=16), :]
        left_ref[:, LANES * r : LANES * r + LANES] = rows
        right_ref[0:MEMBERS, LANES * r : LANES * r + LANES] = rows * weight[r : r + 1]
        right_ref[MEMBERS : MEMBERS + 1, LANES * r : LANES * r + LANES] = aim[r : r + 1]
    gram_ref[...] = lax.dot_general(
        left_ref[...],
        right_ref[...],
        (((1,), (1,)), ((), ())),
        precision=HIGHEST,
        preferred_element_type=jnp.float32,
    )


def fill_coefs(lon, lat, coefs):
    west_c, east_c, south_c, north_c, own_c = coefs
    west_c[...] = jnp.maximum(lon, 0.0)
    east_c[...] = jnp.maximum(-lon, 0.0)
    south_c[...] = jnp.maximum(lat, 0.0)
    north_c[...] = jnp.maximum(-lat, 0.0)
    own_c[...] = jnp.abs(lon) + jnp.abs(lat)


def first_body(mid_ref, low_ref, high_ref, fields_ref, cells_ref, gram_ref, anoms_ref, full_ref, *scratch):
    coefs, rest = scratch[:5], scratch[5:]
    anoms_ref[:, 0:HALO] = low_ref[0:PAIRS]
    anoms_ref[:, HALO : HALO + CY] = mid_ref[...]
    anoms_ref[:, HALO + CY : ROWS] = high_ref[0:PAIRS]
    for index in range(3):
        full_ref[index, 0:HALO] = low_ref[PAIRS + index]
        full_ref[index, HALO : HALO + CY] = fields_ref[index]
        full_ref[index, HALO + CY : ROWS] = high_ref[PAIRS + index]
    fill_coefs(full_ref[1], full_ref[2], coefs)
    observe_and_gram(full_ref[0], anoms_ref, coefs, cells_ref, gram_ref, *rest)


def solve(sums, weights):
    shape = (MEMBERS, LANES)
    lane = lane_of(shape)
    sub = lax.broadcasted_iota(jnp.int32, shape, 0)
    left = MEMBERS - 1.0
    matrix = jnp.where(
        lane < MEMBERS,
        sums + jnp.where(lane == sub, left, 0.0),
        jnp.where(lane == MEMBERS, left * weights - sums, 0.0),
    )
    for k in range(MEMBERS):
        row = matrix[k : k + 1]
        column = jnp.broadcast_to(matrix[:, k : k + 1], shape)
        factor = column / column[k : k + 1]
        matrix = matrix - jnp.where(sub == k, 0.0, factor) * row
    diagonal = jnp.sum(jnp.where(lane == sub, matrix, 0.0), axis=1, keepdims=True)
    solved = matrix[:, MEMBERS : MEMBERS + 1] / diagonal
    return weights - jnp.broadcast_to(solved, shape)


def by_pair(weights):
    lane = lane_of((PAIRS, LANES))
    return jnp.where(lane < 64, weights[0:PAIRS], weights[PAIRS:MEMBERS])


def mix(pair_ref, anoms_ref, low, rows):
    total = jnp.zeros((rows, LANES), jnp.float32)
    for p in range(PAIRS):
        total = total + pair_ref[p : p + 1] * anoms_ref[p, low : low + rows]
    return total + pltpu.roll(total, 64, axis=1)


def second_body(sums_ref, anoms_ref, full_ref, cells_ref, gram_ref, weights_ref, *scratch):
    pair_ref, coefs, rest = scratch[0], scratch[1:6], scratch[6:]
    fill_coefs(full_ref[1], full_ref[2], coefs)
    weights = solve(sums_ref[...], jnp.zeros((MEMBERS, LANES), jnp.float32))
    weights_ref[...] = weights
    pair_ref[...] = by_pair(weights)
    base = full_ref[0] + mix(pair_ref, anoms_ref, 0, ROWS)
    observe_and_gram(base, anoms_ref, coefs, cells_ref, gram_ref, *rest)


def last_body(sums_ref, weights_ref, anoms_ref, out_ref, pair_ref):
    weights = solve(sums_ref[...], weights_ref[...])
    pair_ref[...] = by_pair(weights)
    total = mix(pair_ref, anoms_ref, HALO, CY)
    lane = lane_of((8, LANES))
    out = None
    for group in range(8):
        lev, part = divmod(group, 4)
        moved = pltpu.roll(
            total[8 * part : 8 * part + 8], (CHUNK * group - 32 * lev - HALO) % LANES, axis=1
        )
        out = moved if out is None else jnp.where(lane >= CHUNK * group, moved, out)
    out_ref[...] = out


def spread_body(x_ref, out_ref):
    lane = lane_of((8, LANES))
    for b in range(8):
        pieces = [x_ref[8 * b + k] for k in range(8)]
        for group in range(8):
            lev, part = divmod(group, 4)
            out = None
            for k in range(8):
                moved = pltpu.roll(pieces[k], (CHUNK * (k - group)) % LANES, axis=1)
                out = moved if out is None else jnp.where(lane >= CHUNK * k, moved, out)
            out_ref[lev, 8 * part : 8 * part + 8, LANES * b : LANES * b + LANES] = out


def exchange(array, axes):
    return lax.all_to_all(array, axes, 0, 0, tiled=True)


def to_all(array, axes, count):
    return exchange(jnp.broadcast_to(array[None], (count, *array.shape)), axes)


def sum_everywhere(gram):
    part = jnp.sum(exchange(gram.reshape(32, 2, LANES), PLANE), axis=0)
    part = jnp.sum(to_all(part, "z", 16), axis=0)
    return to_all(part, PLANE, 32).reshape(MEMBERS, LANES)


def local(
    background, anomalies, courant_lon, courant_lat, obs_value, obs_weight, obs_column, obs_level
):
    chunk = lax.axis_index(MEM).astype(jnp.int32).reshape(1)
    pieces, fields = call(
        pack_body,
        (f32(MEMBERS, 16, LANES), f32(3, CY, LANES)),
        in_specs=[SMEM] + [VMEM] * 4,
    )(chunk, anomalies[0], background, courant_lon, courant_lat)
    pieces = exchange(pieces, MEM)
    mid, low_edge, high_edge = call(
        pair_body,
        (f32(PAIRS, CY, LANES), f32(PAIRS + 3, HALO, LANES), f32(PAIRS + 3, HALO, LANES)),
        in_specs=[VMEM] * 2,
    )(pieces, fields)
    forward = [(i, i + 1) for i in range(7)]
    backward = [(i + 1, i) for i in range(7)]
    low = lax.ppermute(high_edge, TILE, forward)
    high = lax.ppermute(low_edge, TILE, backward)
    nobs = obs_value.shape[0]
    flat = [a.reshape(1, nobs) for a in (obs_value, obs_weight, obs_column, obs_level)]
    cells = call(cells_body, f32(2, CY, LANES), in_specs=[SMEM] + [VMEM] * 4)(chunk, *flat)
    coefs = [pltpu.VMEM((ROWS, LANES), jnp.float32)] * 5
    rest = [
        pltpu.VMEM((PAIRS, CY, LANES), jnp.float32),
        pltpu.VMEM((MEMBERS * 16, LANES), jnp.float32),
        pltpu.VMEM((MEMBERS, 16 * LANES), jnp.float32),
        pltpu.VMEM((LANES, 16 * LANES), jnp.float32),
    ]
    pair = pltpu.VMEM((PAIRS, LANES), jnp.float32)
    gram, anoms, full = call(
        first_body,
        (f32(MEMBERS, LANES), f32(PAIRS, ROWS, LANES), f32(3, ROWS, LANES)),
        coefs + rest,
        in_specs=[VMEM] * 5,
    )(mid, low, high, fields, cells)
    gram, weights = call(
        second_body,
        (f32(MEMBERS, LANES), f32(MEMBERS, LANES)),
        [pair] + coefs + rest,
        in_specs=[VMEM] * 4,
    )(sum_everywhere(gram), anoms, full, cells)
    part = call(last_body, f32(8, LANES), [pair], in_specs=[VMEM] * 3)(
        sum_everywhere(gram), weights, anoms
    )
    parts = to_all(part, MEM, MEMBERS)
    return call(spread_body, f32(LEV, CY, NX), in_specs=[VMEM])(parts)


def solution(mesh):
    fine = Mesh(mesh.devices.reshape(16, 2, 2, 2, 4), ("z", "yl", "core", "yh", "x"))
    return jax.shard_map(
        local,
        mesh=fine,
        in_specs=(
            P(None, TILE, None),
            P(MEM, None, TILE, None),
            P(None, TILE, None),
            P(None, TILE, None),
            P(TILE),
            P(TILE),
            P(TILE),
            P(TILE),
        ),
        out_specs=P(None, TILE, None),
        check_vma=False,
    )
```

```python
import functools

import jax
import jax.numpy as jnp
from jax import lax
from jax.experimental import pallas as pl
from jax.experimental.pallas import tpu as pltpu
from jax.sharding import Mesh, PartitionSpec as P

NSTEP = 8
MEMBERS = 64
PAIRS = 32
GROUP = 8
LEV = 2
CY = 32
NX = 1024
CHUNK = 16
HALO = 8
ROWS = CY + 2 * HALO
LANES = 128
HIGHEST = lax.Precision.HIGHEST

MEM = ("z", "yl", "core")
TILE = ("yh", "x")
PLANE = ("yl", "core", "yh", "x")
VMEM = pl.BlockSpec(memory_space=pltpu.VMEM)
SMEM = pl.BlockSpec(memory_space=pltpu.SMEM)


def lane_of(shape):
    return lax.broadcasted_iota(jnp.int32, shape, len(shape) - 1)


def call(body, out, scratch=(), in_specs=None, vmem=40 << 20):
    return pl.pallas_call(
        body,
        out_shape=out,
        in_specs=in_specs,
        out_specs=jax.tree.map(lambda _: VMEM, out),
        scratch_shapes=list(scratch),
        compiler_params=pltpu.CompilerParams(vmem_limit_bytes=vmem),
    )


def f32(*shape):
    return jax.ShapeDtypeStruct(shape, jnp.float32)


def pack_body(own_ref, pieces_ref):
    lane = lane_of((16, LANES))
    shifted = []
    for group in range(4):
        half, lev = divmod(group, 2)
        rolled = [
            pltpu.roll(
                own_ref[lev, 16 * half : 16 * half + 16, LANES * b : LANES * b + LANES],
                HALO,
                axis=1,
            )
            for b in range(8)
        ]
        shifted.append([jnp.where(lane < HALO, rolled[b - 1], rolled[b]) for b in range(8)])
    for b in range(8):
        for k in range(8):
            out = None
            for group in range(4):
                amount = (32 * group - CHUNK * k) % LANES
                source = shifted[group][b]
                if k == 7:
                    source = jnp.where(lane < CHUNK, shifted[group][(b + 1) % 8], source)
                moved = pltpu.roll(source, amount, axis=1) if amount else source
                out = moved if out is None else jnp.where(lane >= 32 * group, moved, out)
            pieces_ref[8 * b + k] = out


def own_fields(chunk_ref, refs, fields_ref):
    chunk = chunk_ref[0]
    b, k = chunk // 8, chunk % 8
    wide = lane_of((CY, LANES))

    def block(ref, lev, index):
        return ref[lev, :, pl.ds(pl.multiple_of(index * LANES, LANES), LANES)]

    for index, ref in enumerate(refs):
        out = None
        for lev in range(LEV):
            mid = block(ref, lev, b)
            low = block(ref, lev, (b + 7) % 8)
            high = block(ref, lev, (b + 1) % 8)
            mid = jnp.where((wide >= LANES - HALO) & (k == 0), low, mid)
            mid = jnp.where((wide < HALO) & (k == 7), high, mid)
            moved = pltpu.roll(mid, (32 * lev + HALO - CHUNK * k + LANES) % LANES, axis=1)
            out = moved if out is None else jnp.where(wide >= 32, moved, out)
        out = jnp.where(wide < 64, out, pltpu.roll(out, 64, axis=1))
        fields_ref[index] = out


def pair_body(chunk_ref, x_ref, bg_ref, lon_ref, lat_ref, fields_ref, mid_ref, low_ref, high_ref):
    own_fields(chunk_ref, (bg_ref, lon_ref, lat_ref), fields_ref)
    lane = lane_of((16, LANES))
    for p in range(PAIRS):
        first, second = x_ref[p], x_ref[p + PAIRS]
        upper = jnp.where(lane < 64, first, pltpu.roll(second, 64, axis=1))
        lower = jnp.where(lane < 64, pltpu.roll(first, 64, axis=1), second)
        mid_ref[p, 0:16] = upper
        mid_ref[p, 16:32] = lower
        low_ref[p] = upper[0:HALO]
        high_ref[p] = lower[HALO:16]
    for index in range(3):
        low_ref[PAIRS + index] = fields_ref[index, 0:HALO]
        high_ref[PAIRS + index] = fields_ref[index, CY - HALO : CY]


def cells_body(chunk_ref, value_ref, weight_ref, column_ref, level_ref, out_ref):
    chunk = chunk_ref[0]
    column = column_ref[...]
    row = column // NX
    offset = column % NX - CHUNK * chunk
    inside = (offset >= 0) & (offset < CHUNK)
    lane = jnp.where(inside, level_ref[...] * 32 + HALO + offset, -1)
    square = weight_ref[...] * weight_ref[...]
    nobs = column.shape[1]
    at_row = lax.broadcasted_iota(jnp.int32, (CY, nobs), 0) == row
    at_lane = (lax.broadcasted_iota(jnp.int32, (LANES, nobs), 0) == lane).astype(jnp.bfloat16)
    parts = []
    for value in (square, square * value_ref[...]):
        left = jnp.where(at_row, value, 0.0)
        for _ in range(3):
            part = left.astype(jnp.bfloat16)
            parts.append(part)
            left = left - part.astype(jnp.float32)
    sums = lax.dot_general(
        jnp.concatenate(parts, axis=0),
        at_lane,
        (((1,), (1,)), ((), ())),
        preferred_element_type=jnp.float32,
    )
    for index in range(2):
        base = 3 * CY * index
        total = sums[base : base + CY] + sums[base + CY : base + 2 * CY]
        total = total + sums[base + 2 * CY : base + 3 * CY]
        out_ref[index] = total


def transport(base, anoms_ref, coefs, buf_ref, first, use):
    west_c, east_c, south_c, north_c, own_c = coefs
    for p in range(GROUP):
        buf_ref[0, p, HALO : HALO + ROWS] = base + 0.5 * anoms_ref[first + p]
    for step in range(NSTEP):
        low, count = (0, ROWS) if step < NSTEP - 1 else (HALO, CY)
        rows = slice(low, low + count)
        at = HALO + low
        for p in range(GROUP):
            now = buf_ref.at[step % 2, p]
            state = now[at : at + count]
            south = now[at - 1 : at - 1 + count]
            north = now[at + 1 : at + 1 + count]
            west = pltpu.roll(state, 1, axis=1)
            east = pltpu.roll(state, LANES - 1, axis=1)
            speed = 0.85 + 0.15 * jnp.tanh(state)
            change = west_c[rows] * west + east_c[rows] * east
            change = change + (south_c[rows] * south + north_c[rows] * north)
            state = state + speed * (change - own_c[rows] * state)
            if step < NSTEP - 1:
                buf_ref[(step + 1) % 2, p, at : at + count] = state
            else:
                use(first + p, state)


def observe_and_gram(
    base, anoms_ref, coefs, cells_ref, gram_ref, buf_ref, total_ref, obs_ref, dev_ref, left_ref, right_ref
):
    edge = jnp.zeros((2, GROUP, HALO, LANES), jnp.float32)
    buf_ref[:, :, 0:HALO] = edge
    buf_ref[:, :, HALO + ROWS :] = edge
    total_ref[...] = jnp.zeros((CY, LANES), jnp.float32)

    def use(p, state):
        seen = state + 0.25 * state * state
        obs_ref[p] = seen
        total_ref[...] += seen

    def one(index, carry):
        transport(base, anoms_ref, coefs, buf_ref, index * GROUP, use)
        return carry

    lax.fori_loop(0, PAIRS // GROUP, one, 0)
    total = total_ref[...]
    center = (total + pltpu.roll(total, 64, axis=1)) * (1.0 / MEMBERS)
    lane = lane_of((16, LANES))
    for p in range(PAIRS):
        dev = obs_ref[p] - center
        upper, lower = dev[0:16], dev[16:32]
        dev_ref[16 * p : 16 * p + 16] = jnp.where(lane < 64, upper, pltpu.roll(lower, 64, axis=1))
        at = 16 * (p + PAIRS)
        dev_ref[at : at + 16] = jnp.where(lane < 64, pltpu.roll(upper, 64, axis=1), lower)
    weight, weighted = cells_ref[0], cells_ref[1]
    aim = 2.0 * (weighted - weight * center)
    aim = jnp.where(lane < 64, aim[0:16], pltpu.roll(aim[16:32], 64, axis=1))
    weight = 4.0 * weight
    weight = jnp.where(lane < 64, weight[0:16], pltpu.roll(weight[16:32], 64, axis=1))
    right_ref[MEMBERS:LANES, :] = jnp.zeros((LANES - MEMBERS, 16 * LANES), jnp.float32)
    for r in range(16):
        rows = dev_ref[pl.ds(r, MEMBERS, stride=16), :]
        left_ref[:, LANES * r : LANES * r + LANES] = rows
        right_ref[0:MEMBERS, LANES * r : LANES * r + LANES] = rows * weight[r : r + 1]
        right_ref[MEMBERS : MEMBERS + 1, LANES * r : LANES * r + LANES] = aim[r : r + 1]
    gram = lax.dot_general(
        left_ref[...],
        right_ref[...],
        (((1,), (1,)), ((), ())),
        precision=HIGHEST,
        preferred_element_type=jnp.float32,
    )
    lane = lane_of((PAIRS, LANES))
    top, bottom = gram[0:PAIRS], gram[PAIRS:MEMBERS]
    ends = jnp.where(lane == 96, pltpu.roll(top, 32, axis=1), pltpu.roll(bottom, 33, axis=1))
    ends = jnp.where(lane < 96, pltpu.roll(bottom, 32, axis=1), ends)
    gram_ref[...] = jnp.where(lane < 64, top, ends)


def fill_coefs(lon, lat, coefs):
    west_c, east_c, south_c, north_c, own_c = coefs
    west_c[...] = jnp.maximum(lon, 0.0)
    east_c[...] = jnp.maximum(-lon, 0.0)
    south_c[...] = jnp.maximum(lat, 0.0)
    north_c[...] = jnp.maximum(-lat, 0.0)
    own_c[...] = jnp.abs(lon) + jnp.abs(lat)


def first_body(mid_ref, low_ref, high_ref, fields_ref, cells_ref, gram_ref, anoms_ref, full_ref, *scratch):
    coefs, rest = scratch[:5], scratch[5:]
    anoms_ref[:, 0:HALO] = low_ref[0:PAIRS]
    anoms_ref[:, HALO : HALO + CY] = mid_ref[...]
    anoms_ref[:, HALO + CY : ROWS] = high_ref[0:PAIRS]
    for index in range(3):
        full_ref[index, 0:HALO] = low_ref[PAIRS + index]
        full_ref[index, HALO : HALO + CY] = fields_ref[index]
        full_ref[index, HALO + CY : ROWS] = high_ref[PAIRS + index]
    fill_coefs(full_ref[1], full_ref[2], coefs)
    observe_and_gram(full_ref[0], anoms_ref, coefs, cells_ref, gram_ref, *rest)


def solve(packed, weights):
    shape = (MEMBERS, LANES)
    lane = lane_of(shape)
    sub = lax.broadcasted_iota(jnp.int32, shape, 0)
    left = MEMBERS - 1.0
    half = lane[0:PAIRS]
    moved = pltpu.roll(packed, LANES - 32, axis=1)
    whole = jnp.concatenate([packed, jnp.zeros((LANES - PAIRS, LANES), jnp.float32)], axis=0)
    cross = jnp.transpose(whole)[32:64]
    bottom = jnp.where(half < 64, moved, pltpu.roll(packed, LANES - 33, axis=1))
    bottom = jnp.where(half < 32, cross, bottom)
    sums = jnp.concatenate([jnp.where(half < 64, packed, moved), bottom], axis=0)
    matrix = jnp.where(
        lane < MEMBERS,
        sums + jnp.where(lane == sub, left, 0.0),
        jnp.where(lane == MEMBERS, left * weights - sums, 0.0),
    )
    width = 8
    for start in range(0, MEMBERS, width):
        columns = [
            jnp.broadcast_to(matrix[:, start + j : start + j + 1], shape) for j in range(width)
        ]
        for j in range(width):
            k = start + j
            factor = jnp.where(sub == k, 0.0, columns[j] * (1.0 / columns[j][k : k + 1]))
            for later in range(j + 1, width):
                columns[later] = columns[later] - factor * columns[later][k : k + 1]
            matrix = matrix - factor * matrix[k : k + 1]
    diagonal = jnp.sum(jnp.where(lane == sub, matrix, 0.0), axis=1, keepdims=True)
    solved = matrix[:, MEMBERS : MEMBERS + 1] / diagonal
    return weights - jnp.broadcast_to(solved, shape)


def by_pair(weights):
    lane = lane_of((PAIRS, LANES))
    return jnp.where(lane < 64, weights[0:PAIRS], weights[PAIRS:MEMBERS])


def mix(pair_ref, anoms_ref, low, rows):
    total = jnp.zeros((rows, LANES), jnp.float32)
    for p in range(PAIRS):
        total = total + pair_ref[p : p + 1] * anoms_ref[p, low : low + rows]
    return total + pltpu.roll(total, 64, axis=1)


def second_body(sums_ref, anoms_ref, full_ref, cells_ref, gram_ref, weights_ref, *scratch):
    pair_ref, coefs, rest = scratch[0], scratch[1:6], scratch[6:]
    fill_coefs(full_ref[1], full_ref[2], coefs)
    weights = solve(sums_ref[...], jnp.zeros((MEMBERS, LANES), jnp.float32))
    weights_ref[...] = weights
    pair_ref[...] = by_pair(weights)
    base = full_ref[0] + mix(pair_ref, anoms_ref, 0, ROWS)
    observe_and_gram(base, anoms_ref, coefs, cells_ref, gram_ref, *rest)


def last_body(sums_ref, weights_ref, anoms_ref, out_ref, pair_ref):
    weights = solve(sums_ref[...], weights_ref[...])
    pair_ref[...] = by_pair(weights)
    total = mix(pair_ref, anoms_ref, HALO, CY)
    lane = lane_of((8, LANES))
    out = None
    for group in range(8):
        lev, part = divmod(group, 4)
        moved = pltpu.roll(
            total[8 * part : 8 * part + 8], (CHUNK * group - 32 * lev - HALO) % LANES, axis=1
        )
        out = moved if out is None else jnp.where(lane >= CHUNK * group, moved, out)
    out_ref[...] = out


def spread_body(x_ref, out_ref):
    lane = lane_of((8, LANES))
    for b in range(8):
        pieces = [x_ref[8 * b + k] for k in range(8)]
        for group in range(8):
            lev, part = divmod(group, 4)
            out = None
            for k in range(8):
                moved = pltpu.roll(pieces[k], (CHUNK * (k - group)) % LANES, axis=1)
                out = moved if out is None else jnp.where(lane >= CHUNK * k, moved, out)
            out_ref[lev, 8 * part : 8 * part + 8, LANES * b : LANES * b + LANES] = out


def exchange(array, axes):
    return lax.all_to_all(array, axes, 0, 0, tiled=True)


def to_all(array, axes, count):
    return exchange(jnp.broadcast_to(array[None], (count, *array.shape)), axes)


def sum_everywhere(packed):
    quarters = jnp.broadcast_to(packed.reshape(4, 1, 8, LANES), (4, 8, 8, LANES))
    part = jnp.sum(exchange(quarters.reshape(32, 8, LANES), PLANE), axis=0)
    part = jnp.sum(to_all(part, "z", 16), axis=0)
    return to_all(part, ("yl", "core"), 4).reshape(PAIRS, LANES)


def local(
    background, anomalies, courant_lon, courant_lat, obs_value, obs_weight, obs_column, obs_level
):
    chunk = lax.axis_index(MEM).astype(jnp.int32).reshape(1)
    pieces = call(pack_body, f32(MEMBERS, 16, LANES), in_specs=[VMEM])(anomalies[0])
    pieces = exchange(pieces, MEM)
    fields, mid, low_edge, high_edge = call(
        pair_body,
        (
            f32(3, CY, LANES),
            f32(PAIRS, CY, LANES),
            f32(PAIRS + 3, HALO, LANES),
            f32(PAIRS + 3, HALO, LANES),
        ),
        in_specs=[SMEM] + [VMEM] * 4,
    )(chunk, pieces, background, courant_lon, courant_lat)
    forward = [(i, i + 1) for i in range(7)]
    backward = [(i + 1, i) for i in range(7)]
    low = lax.ppermute(high_edge, TILE, forward)
    high = lax.ppermute(low_edge, TILE, backward)
    nobs = obs_value.shape[0]
    flat = [a.reshape(1, nobs) for a in (obs_value, obs_weight, obs_column, obs_level)]
    cells = call(cells_body, f32(2, CY, LANES), in_specs=[SMEM] + [VMEM] * 4)(chunk, *flat)
    coefs = [pltpu.VMEM((ROWS, LANES), jnp.float32)] * 5
    rest = [
        pltpu.VMEM((2, GROUP, ROWS + 2 * HALO, LANES), jnp.float32),
        pltpu.VMEM((CY, LANES), jnp.float32),
        pltpu.VMEM((PAIRS, CY, LANES), jnp.float32),
        pltpu.VMEM((MEMBERS * 16, LANES), jnp.float32),
        pltpu.VMEM((MEMBERS, 16 * LANES), jnp.float32),
        pltpu.VMEM((LANES, 16 * LANES), jnp.float32),
    ]
    pair = pltpu.VMEM((PAIRS, LANES), jnp.float32)
    gram, anoms, full = call(
        first_body,
        (f32(PAIRS, LANES), f32(PAIRS, ROWS, LANES), f32(3, ROWS, LANES)),
        coefs + rest,
        in_specs=[VMEM] * 5,
    )(mid, low, high, fields, cells)
    gram, weights = call(
        second_body,
        (f32(PAIRS, LANES), f32(MEMBERS, LANES)),
        [pair] + coefs + rest,
        in_specs=[VMEM] * 4,
    )(sum_everywhere(gram), anoms, full, cells)
    part = call(last_body, f32(8, LANES), [pair], in_specs=[VMEM] * 3)(
        sum_everywhere(gram), weights, anoms
    )
    parts = to_all(part, MEM, MEMBERS)
    return call(spread_body, f32(LEV, CY, NX), in_specs=[VMEM])(parts)


def solution(mesh):
    fine = Mesh(mesh.devices.reshape(16, 2, 2, 2, 4), ("z", "yl", "core", "yh", "x"))
    return jax.shard_map(
        local,
        mesh=fine,
        in_specs=(
            P(None, TILE, None),
            P(MEM, None, TILE, None),
            P(None, TILE, None),
            P(None, TILE, None),
            P(TILE),
            P(TILE),
            P(TILE),
            P(TILE),
        ),
        out_specs=P(None, TILE, None),
        check_vma=False,
    )
```

```python
import functools

import jax
import jax.numpy as jnp
from jax import lax
from jax.experimental import pallas as pl
from jax.experimental.pallas import tpu as pltpu
from jax.sharding import Mesh, PartitionSpec as P

NSTEP = 8
MEMBERS = 64
PAIRS = 32
GROUP = 8
LEV = 2
CY = 32
NX = 1024
CHUNK = 32
HALO = 8
ROWS = CY + 2 * HALO
LANES = 128
PACKED = 20
HIGHEST = lax.Precision.HIGHEST

MEM = ("z", "yl", "core")
TILE = ("yh", "x")
PLANE = ("yl", "core", "yh", "x")
VMEM = pl.BlockSpec(memory_space=pltpu.VMEM)
SMEM = pl.BlockSpec(memory_space=pltpu.SMEM)


def lane_of(shape):
    return lax.broadcasted_iota(jnp.int32, shape, len(shape) - 1)


def call(body, out, scratch=(), in_specs=None, vmem=40 << 20):
    return pl.pallas_call(
        body,
        out_shape=out,
        in_specs=in_specs,
        out_specs=jax.tree.map(lambda _: VMEM, out),
        scratch_shapes=list(scratch),
        compiler_params=pltpu.CompilerParams(vmem_limit_bytes=vmem),
    )


def f32(*shape):
    return jax.ShapeDtypeStruct(shape, jnp.float32)


def pack_body(own_ref, pieces_ref):
    lane = lane_of((8, LANES))
    for lev in range(LEV):
        turned = []
        for q in range(4):
            rolled = [
                pltpu.roll(own_ref[lev, 8 * q : 8 * q + 8, LANES * b : LANES * b + LANES], HALO, axis=1)
                for b in range(8)
            ]
            shifted = [jnp.where(lane < HALO, rolled[b - 1], rolled[b]) for b in range(8)]
            turned.append(
                [
                    [pltpu.roll(block, 32 * n, axis=1) if n else block for n in range(4)]
                    for block in shifted
                ]
            )

        def gather(b, k):
            out = turned[0][b][(-k) % 4]
            for q in range(1, 4):
                out = jnp.where(lane >= 32 * q, turned[q][b][(q - k) % 4], out)
            return out

        for b in range(8):
            for k in range(4):
                at = 12 * (32 * lev + 4 * b + k)
                pieces_ref[at : at + 8] = gather(b, k)
                rest = gather(b, k + 1) if k < 3 else gather((b + 1) % 8, 0)
                other = pltpu.roll(rest, 16, axis=1)
                pieces_ref[at + 8 : at + 12] = jnp.where(
                    lane[0:4] % 32 < 16, rest[0:4], other[4:8]
                )


def own_fields(chunk_ref, refs, fields_ref):
    chunk = chunk_ref[0]
    lev, b, k = chunk // 32, chunk % 32 // 4, chunk % 4
    wide = lane_of((CY, LANES))

    def block(ref, index):
        return ref[lev, :, pl.ds(pl.multiple_of(index * LANES, LANES), LANES)]

    for index, ref in enumerate(refs):
        mid = block(ref, b)
        mid = jnp.where((wide >= LANES - HALO) & (k == 0), block(ref, (b + 7) % 8), mid)
        mid = jnp.where((wide < HALO) & (k == 3), block(ref, (b + 1) % 8), mid)
        mid = pltpu.roll(mid, (HALO - CHUNK * k + LANES) % LANES, axis=1)
        mid = jnp.where(wide < CHUNK + 2 * HALO, mid, 0.0)
        fields_ref[index] = jnp.where(wide < 64, mid, pltpu.roll(mid, 64, axis=1))


def pair_body(chunk_ref, x_ref, bg_ref, lon_ref, lat_ref, fields_ref, mid_ref, low_ref, high_ref):
    own_fields(chunk_ref, (bg_ref, lon_ref, lat_ref), fields_ref)
    lane = lane_of((8, LANES))
    place = lane % 64

    def one(p, carry):
        parts = []
        for member in (p, p + PAIRS):
            main = x_ref[pl.ds(12 * member, 8)]
            rest = x_ref[pl.ds(12 * member + 8, 4)]
            parts.append((main, jnp.concatenate([rest, pltpu.roll(rest, LANES - 16, axis=1)], axis=0)))
        for q in range(4):
            out = None
            for half, (main, rest) in enumerate(parts):
                moved = pltpu.roll(main, (64 * half - 32 * q) % LANES, axis=1)
                tail = pltpu.roll(rest, (64 * half + 32 - 32 * q) % LANES, axis=1)
                moved = jnp.where(place < 32, moved, tail)
                out = moved if out is None else jnp.where(lane < 64, out, moved)
            out = jnp.where(place < CHUNK + 2 * HALO, out, 0.0)
            mid_ref[p, 8 * q : 8 * q + 8] = out
            if q == 0:
                low_ref[p] = out
            if q == 3:
                high_ref[p] = out
        return carry

    lax.fori_loop(0, PAIRS, one, 0, unroll=4)
    for index in range(3):
        low_ref[PAIRS + index] = fields_ref[index, 0:HALO]
        high_ref[PAIRS + index] = fields_ref[index, CY - HALO : CY]


def cells_body(chunk_ref, value_ref, weight_ref, column_ref, level_ref, out_ref):
    chunk = chunk_ref[0]
    column = column_ref[...]
    row = column // NX
    offset = column % NX - CHUNK * (chunk % 32)
    inside = (offset >= 0) & (offset < CHUNK) & (level_ref[...] == chunk // 32)
    lane = jnp.where(inside, HALO + offset, -1)
    square = weight_ref[...] * weight_ref[...]
    nobs = column.shape[1]
    at_row = lax.broadcasted_iota(jnp.int32, (CY, nobs), 0) == row
    at_lane = (lax.broadcasted_iota(jnp.int32, (LANES, nobs), 0) == lane).astype(jnp.bfloat16)
    parts = []
    for value in (square, square * value_ref[...]):
        left = jnp.where(at_row, value, 0.0)
        for _ in range(3):
            part = left.astype(jnp.bfloat16)
            parts.append(part)
            left = left - part.astype(jnp.float32)
    sums = lax.dot_general(
        jnp.concatenate(parts, axis=0),
        at_lane,
        (((1,), (1,)), ((), ())),
        preferred_element_type=jnp.float32,
    )
    for index in range(2):
        base = 3 * CY * index
        total = sums[base : base + CY] + sums[base + CY : base + 2 * CY]
        total = total + sums[base + 2 * CY : base + 3 * CY]
        out_ref[index] = total


def transport(base, anoms_ref, coefs, buf_ref, first, use):
    west_c, east_c, south_c, north_c, own_c = coefs
    for p in range(GROUP):
        buf_ref[0, p, HALO : HALO + ROWS] = base + 0.5 * anoms_ref[first + p]
    for step in range(NSTEP):
        low, count = (0, ROWS) if step < NSTEP - 1 else (HALO, CY)
        rows = slice(low, low + count)
        at = HALO + low
        for p in range(GROUP):
            now = buf_ref.at[step % 2, p]
            state = now[at : at + count]
            south = now[at - 1 : at - 1 + count]
            north = now[at + 1 : at + 1 + count]
            west = pltpu.roll(state, 1, axis=1)
            east = pltpu.roll(state, LANES - 1, axis=1)
            speed = 0.85 + 0.15 * jnp.tanh(state)
            change = west_c[rows] * west + east_c[rows] * east
            change = change + (south_c[rows] * south + north_c[rows] * north)
            state = state + speed * (change - own_c[rows] * state)
            if step < NSTEP - 1:
                buf_ref[(step + 1) % 2, p, at : at + count] = state
            else:
                use(first + p, state)


def inner(rows, start):
    lane = lane_of((8, LANES))
    out = None
    for q in range(4):
        moved = pltpu.roll(rows[8 * q : 8 * q + 8], (32 * q - HALO - start) % LANES, axis=1)
        out = moved if out is None else jnp.where(lane >= 32 * q, moved, out)
    return out


def observe_and_gram(
    base, anoms_ref, coefs, cells_ref, gram_ref, buf_ref, total_ref, obs_ref, dev_ref, left_ref, right_ref
):
    edge = jnp.zeros((2, GROUP, HALO, LANES), jnp.float32)
    buf_ref[:, :, 0:HALO] = edge
    buf_ref[:, :, HALO + ROWS :] = edge
    total_ref[...] = jnp.zeros((CY, LANES), jnp.float32)

    def use(p, state):
        seen = state + 0.25 * state * state
        obs_ref[p] = seen
        total_ref[...] += seen

    def one(index, carry):
        transport(base, anoms_ref, coefs, buf_ref, index * GROUP, use)
        return carry

    lax.fori_loop(0, PAIRS // GROUP, one, 0)
    total = total_ref[...]
    center = (total + pltpu.roll(total, 64, axis=1)) * (1.0 / MEMBERS)
    for p in range(PAIRS):
        dev = obs_ref[p] - center
        for half in range(2):
            at = 8 * (p + PAIRS * half)
            dev_ref[at : at + 8] = inner(dev, 64 * half)
    weight, weighted = cells_ref[0], cells_ref[1]
    aim = inner(2.0 * (weighted - weight * center), 0)
    weight = inner(4.0 * weight, 0)
    right_ref[MEMBERS:LANES, :] = jnp.zeros((LANES - MEMBERS, 8 * LANES), jnp.float32)
    for r in range(8):
        rows = dev_ref[pl.ds(r, MEMBERS, stride=8), :]
        left_ref[:, LANES * r : LANES * r + LANES] = rows
        right_ref[0:MEMBERS, LANES * r : LANES * r + LANES] = rows * weight[r : r + 1]
        right_ref[MEMBERS : MEMBERS + 1, LANES * r : LANES * r + LANES] = aim[r : r + 1]
    gram = lax.dot_general(
        left_ref[...],
        right_ref[...],
        (((1,), (1,)), ((), ())),
        precision=HIGHEST,
        preferred_element_type=jnp.float32,
    )
    wide = lane_of((MEMBERS, LANES))
    sub = lax.broadcasted_iota(jnp.int32, (MEMBERS, LANES), 0)
    column = jnp.broadcast_to(gram[:, MEMBERS : MEMBERS + 1], (MEMBERS, LANES))
    project = jnp.sum(jnp.where(wide == sub, column, 0.0), axis=0, keepdims=True)
    top, bottom = gram[0:PAIRS], gram[PAIRS:MEMBERS]
    lane, sub = wide[0:PAIRS], sub[0:PAIRS]
    diagonal = jnp.sum(jnp.where(lane - 32 == sub, bottom, 0.0), axis=0, keepdims=True)
    square = jnp.where(lane - 32 >= sub, pltpu.roll(top, 32, axis=1), bottom)
    square = jnp.where(lane < 32, pltpu.roll(top, LANES - 32, axis=1), square)
    packed = jnp.where(lane[0:16] < 64, square[0:16], pltpu.roll(square[16:32], 64, axis=1))
    gram_ref[...] = jnp.zeros((PACKED, LANES), jnp.float32)
    gram_ref[0:8] = packed[0:8]
    gram_ref[8:9] = jnp.where(lane[0:1] < 64, project, pltpu.roll(diagonal, 32, axis=1))
    gram_ref[10:18] = packed[8:16]


def fill_coefs(lon, lat, coefs):
    west_c, east_c, south_c, north_c, own_c = coefs
    west_c[...] = jnp.maximum(lon, 0.0)
    east_c[...] = jnp.maximum(-lon, 0.0)
    south_c[...] = jnp.maximum(lat, 0.0)
    north_c[...] = jnp.maximum(-lat, 0.0)
    own_c[...] = jnp.abs(lon) + jnp.abs(lat)


def first_body(mid_ref, low_ref, high_ref, fields_ref, cells_ref, gram_ref, anoms_ref, full_ref, *scratch):
    coefs, rest = scratch[:5], scratch[5:]
    anoms_ref[:, 0:HALO] = low_ref[0:PAIRS]
    anoms_ref[:, HALO : HALO + CY] = mid_ref[...]
    anoms_ref[:, HALO + CY : ROWS] = high_ref[0:PAIRS]
    for index in range(3):
        full_ref[index, 0:HALO] = low_ref[PAIRS + index]
        full_ref[index, HALO : HALO + CY] = fields_ref[index]
        full_ref[index, HALO + CY : ROWS] = high_ref[PAIRS + index]
    fill_coefs(full_ref[1], full_ref[2], coefs)
    observe_and_gram(full_ref[0], anoms_ref, coefs, cells_ref, gram_ref, *rest)


def solve(core, own, other, weights):
    shape = (MEMBERS, LANES)
    wide = lane_of(shape)
    sub = lax.broadcasted_iota(jnp.int32, shape, 0)
    left = MEMBERS - 1.0
    low, high = jnp.where(core == 0, own, other), jnp.where(core == 0, other, own)
    packed = jnp.concatenate([low[0:8], high[0:8]], axis=0)
    ends = jnp.broadcast_to(low[8:9], shape)
    square = jnp.concatenate([packed, pltpu.roll(packed, 64, axis=1)], axis=0)
    padded = jnp.concatenate([square, jnp.zeros((LANES - PAIRS, LANES), jnp.float32)], axis=0)
    turned = jnp.transpose(padded)
    lane, row = wide[0:PAIRS], sub[0:PAIRS]
    top = jnp.where(lane >= row, pltpu.roll(square, LANES - 32, axis=1), turned[32:64])
    top = jnp.where(lane < 32, top, pltpu.roll(square, 32, axis=1))
    bottom = jnp.where(lane - 32 < row, square, pltpu.roll(turned[32:64], 32, axis=1))
    bottom = jnp.where(lane - 32 == row, pltpu.roll(ends, LANES - 32, axis=1)[0:PAIRS], bottom)
    bottom = jnp.where(lane < 32, turned[0:32], bottom)
    sums = jnp.concatenate([top, bottom], axis=0)
    project = jnp.sum(jnp.where(wide == sub, ends, 0.0), axis=1, keepdims=True)
    gradient = left * weights - jnp.broadcast_to(project, shape)
    lane = wide
    matrix = jnp.where(
        lane < MEMBERS,
        sums + jnp.where(lane == sub, left, 0.0),
        jnp.where(lane == MEMBERS, gradient, 0.0),
    )
    width = 8
    for start in range(0, MEMBERS, width):
        columns = [
            jnp.broadcast_to(matrix[:, start + j : start + j + 1], shape) for j in range(width)
        ]
        for j in range(width):
            k = start + j
            factor = jnp.where(sub == k, 0.0, columns[j] * (1.0 / columns[j][k : k + 1]))
            for later in range(j + 1, width):
                columns[later] = columns[later] - factor * columns[later][k : k + 1]
            matrix = matrix - factor * matrix[k : k + 1]
    diagonal = jnp.sum(jnp.where(lane == sub, matrix, 0.0), axis=1, keepdims=True)
    solved = matrix[:, MEMBERS : MEMBERS + 1] / diagonal
    return weights - jnp.broadcast_to(solved, shape)


def by_pair(weights):
    lane = lane_of((PAIRS, LANES))
    return jnp.where(lane < 64, weights[0:PAIRS], weights[PAIRS:MEMBERS])


def mix(pair_ref, anoms_ref, low, rows):
    total = jnp.zeros((rows, LANES), jnp.float32)
    for p in range(PAIRS):
        total = total + pair_ref[p : p + 1] * anoms_ref[p, low : low + rows]
    return total + pltpu.roll(total, 64, axis=1)


def second_body(core_ref, own_ref, other_ref, anoms_ref, full_ref, cells_ref, gram_ref, weights_ref, *scratch):
    pair_ref, coefs, rest = scratch[0], scratch[1:6], scratch[6:]
    fill_coefs(full_ref[1], full_ref[2], coefs)
    weights = solve(
        core_ref[0], own_ref[...], other_ref[...], jnp.zeros((MEMBERS, LANES), jnp.float32)
    )
    weights_ref[...] = weights
    pair_ref[...] = by_pair(weights)
    base = full_ref[0] + mix(pair_ref, anoms_ref, 0, ROWS)
    observe_and_gram(base, anoms_ref, coefs, cells_ref, gram_ref, *rest)


def last_body(core_ref, own_ref, other_ref, weights_ref, anoms_ref, out_ref, pair_ref):
    weights = solve(core_ref[0], own_ref[...], other_ref[...], weights_ref[...])
    pair_ref[...] = by_pair(weights)
    out_ref[...] = inner(mix(pair_ref, anoms_ref, HALO, CY), 0)


def spread_body(core_ref, own_ref, other_ref, out_ref):
    lane = lane_of((8, LANES))
    first = core_ref[0] == 0
    for lev in range(LEV):
        for b in range(8):
            pieces = []
            for k in range(4):
                at = 16 * lev + 2 * b + k // 2
                own, other = own_ref[at], other_ref[at]
                if k % 2:
                    own, other = other, own
                pieces.append(jnp.where(first, own, other))
            for q in range(4):
                out = None
                for k in range(4):
                    moved = pltpu.roll(pieces[k], (32 * (k - q)) % LANES, axis=1)
                    out = moved if out is None else jnp.where(lane >= 32 * k, moved, out)
                out_ref[lev, 8 * q : 8 * q + 8, LANES * b : LANES * b + LANES] = out


def exchange(array, axes):
    return lax.all_to_all(array, axes, 0, 0, tiled=True)


def to_all(array, axes, count):
    return exchange(jnp.broadcast_to(array[None], (count, *array.shape)), axes)


def swap_cores(array):
    return lax.ppermute(array, "core", [(0, 1), (1, 0)])


def sum_everywhere(packed):
    shape = (5, 2, LANES)
    halves = jnp.broadcast_to(packed.reshape(1, 2, 1, *shape), (2, 2, 8, *shape))
    part = jnp.sum(exchange(halves.reshape(32, *shape), PLANE), axis=0)
    part = jnp.sum(to_all(part, "z", 16), axis=0).reshape(10, LANES)
    return part, swap_cores(part)


def local(
    background, anomalies, courant_lon, courant_lat, obs_value, obs_weight, obs_column, obs_level
):
    chunk = lax.axis_index(MEM).astype(jnp.int32).reshape(1)
    core = lax.axis_index("core").astype(jnp.int32).reshape(1)
    pieces = call(pack_body, f32(MEMBERS * 12, LANES), in_specs=[VMEM])(anomalies[0])
    pieces = exchange(pieces.reshape(MEMBERS, 3, 4, LANES), MEM).reshape(MEMBERS * 12, LANES)
    fields, mid, low_edge, high_edge = call(
        pair_body,
        (
            f32(3, CY, LANES),
            f32(PAIRS, CY, LANES),
            f32(PAIRS + 3, HALO, LANES),
            f32(PAIRS + 3, HALO, LANES),
        ),
        in_specs=[SMEM] + [VMEM] * 4,
    )(chunk, pieces, background, courant_lon, courant_lat)
    forward = [(i, i + 1) for i in range(7)]
    backward = [(i + 1, i) for i in range(7)]
    low = lax.ppermute(high_edge, TILE, forward)
    high = lax.ppermute(low_edge, TILE, backward)
    nobs = obs_value.shape[0]
    flat = [a.reshape(1, nobs) for a in (obs_value, obs_weight, obs_column, obs_level)]
    cells = call(cells_body, f32(2, CY, LANES), in_specs=[SMEM] + [VMEM] * 4)(chunk, *flat)
    coefs = [pltpu.VMEM((ROWS, LANES), jnp.float32)] * 5
    rest = [
        pltpu.VMEM((2, GROUP, ROWS + 2 * HALO, LANES), jnp.float32),
        pltpu.VMEM((CY, LANES), jnp.float32),
        pltpu.VMEM((PAIRS, CY, LANES), jnp.float32),
        pltpu.VMEM((MEMBERS * 8, LANES), jnp.float32),
        pltpu.VMEM((MEMBERS, 8 * LANES), jnp.float32),
        pltpu.VMEM((LANES, 8 * LANES), jnp.float32),
    ]
    pair = pltpu.VMEM((PAIRS, LANES), jnp.float32)
    gram, anoms, full = call(
        first_body,
        (f32(PACKED, LANES), f32(PAIRS, ROWS, LANES), f32(3, ROWS, LANES)),
        coefs + rest,
        in_specs=[VMEM] * 5,
    )(mid, low, high, fields, cells)
    gram, weights = call(
        second_body,
        (f32(PACKED, LANES), f32(MEMBERS, LANES)),
        [pair] + coefs + rest,
        in_specs=[SMEM] + [VMEM] * 5,
    )(core, *sum_everywhere(gram), anoms, full, cells)
    part = call(last_body, f32(8, LANES), [pair], in_specs=[SMEM] + [VMEM] * 4)(
        core, *sum_everywhere(gram), weights, anoms
    )
    parts = to_all(part, ("z", "yl"), 32)
    return call(spread_body, f32(LEV, CY, NX), in_specs=[SMEM] + [VMEM] * 2)(
        core, parts, swap_cores(parts)
    )


def solution(mesh):
    fine = Mesh(mesh.devices.reshape(16, 2, 2, 2, 4), ("z", "yl", "core", "yh", "x"))
    return jax.shard_map(
        local,
        mesh=fine,
        in_specs=(
            P(None, TILE, None),
            P(MEM, None, TILE, None),
            P(None, TILE, None),
            P(None, TILE, None),
            P(TILE),
            P(TILE),
            P(TILE),
            P(TILE),
        ),
        out_specs=P(None, TILE, None),
        check_vma=False,
    )
```

```python
import functools

import jax
import jax.numpy as jnp
from jax import lax
from jax.experimental import pallas as pl
from jax.experimental.pallas import tpu as pltpu
from jax.sharding import Mesh, PartitionSpec as P

NSTEP = 8
MEMBERS = 64
PAIRS = 32
GROUP = 8
LEV = 2
CY = 32
NX = 1024
CHUNK = 32
HALO = 8
ROWS = CY + 2 * HALO
EDGE = 12 * MEMBERS // 4 + 3 * HALO
LANES = 128
PACKED = 20
HIGHEST = lax.Precision.HIGHEST

MEM = ("z", "yl", "core")
TILE = ("yh", "x")
PLANE = ("yl", "core", "yh", "x")
VMEM = pl.BlockSpec(memory_space=pltpu.VMEM)
SMEM = pl.BlockSpec(memory_space=pltpu.SMEM)


def lane_of(shape):
    return lax.broadcasted_iota(jnp.int32, shape, len(shape) - 1)


def call(body, out, scratch=(), in_specs=None, vmem=40 << 20):
    return pl.pallas_call(
        body,
        out_shape=out,
        in_specs=in_specs,
        out_specs=jax.tree.map(lambda _: VMEM, out),
        scratch_shapes=list(scratch),
        compiler_params=pltpu.CompilerParams(vmem_limit_bytes=vmem),
    )


def f32(*shape):
    return jax.ShapeDtypeStruct(shape, jnp.float32)


def pack_body(own_ref, pieces_ref):
    lane = lane_of((8, LANES))
    for lev in range(LEV):
        turned = []
        for q in range(4):
            rolled = [
                pltpu.roll(own_ref[lev, 8 * q : 8 * q + 8, LANES * b : LANES * b + LANES], HALO, axis=1)
                for b in range(8)
            ]
            shifted = [jnp.where(lane < HALO, rolled[b - 1], rolled[b]) for b in range(8)]
            turned.append(
                [
                    [pltpu.roll(block, 32 * n, axis=1) if n else block for n in range(4)]
                    for block in shifted
                ]
            )

        def gather(b, k):
            out = turned[0][b][(-k) % 4]
            for q in range(1, 4):
                out = jnp.where(lane >= 32 * q, turned[q][b][(q - k) % 4], out)
            return out

        for b in range(8):
            for k in range(4):
                at = 12 * (32 * lev + 4 * b + k)
                pieces_ref[at : at + 8] = gather(b, k)
                rest = gather(b, k + 1) if k < 3 else gather((b + 1) % 8, 0)
                other = pltpu.roll(rest, 16, axis=1)
                pieces_ref[at + 8 : at + 12] = jnp.where(
                    lane[0:4] % 32 < 16, rest[0:4], other[4:8]
                )


def fields_body(chunk_ref, bg_ref, lon_ref, lat_ref, fields_ref):
    chunk = chunk_ref[0]
    lev, b, k = chunk // 32, chunk % 32 // 4, chunk % 4
    wide = lane_of((CY, LANES))

    def block(ref, index):
        return ref[lev, :, pl.ds(pl.multiple_of(index * LANES, LANES), LANES)]

    for index, ref in enumerate((bg_ref, lon_ref, lat_ref)):
        mid = block(ref, b)
        mid = jnp.where((wide >= LANES - HALO) & (k == 0), block(ref, (b + 7) % 8), mid)
        mid = jnp.where((wide < HALO) & (k == 3), block(ref, (b + 1) % 8), mid)
        mid = pltpu.roll(mid, (HALO - CHUNK * k + LANES) % LANES, axis=1)
        mid = jnp.where(wide < CHUNK + 2 * HALO, mid, 0.0)
        fields_ref[index] = jnp.where(wide < 64, mid, pltpu.roll(mid, 64, axis=1))


def edges_body(x_ref, fields_ref, low_ref, high_ref):
    lane = lane_of((12, LANES))
    for u in range(MEMBERS // 4):
        low, high = None, None
        for i in range(4):
            at = 12 * (4 * u + i)
            piece = x_ref[at : at + 12]
            first = pltpu.roll(piece, 32 * i, axis=1) if i else piece
            last = pltpu.roll(piece, (32 * i + 32) % LANES, axis=1) if i < 3 else piece
            low = first if i == 0 else jnp.where(lane >= 32 * i, first, low)
            high = last if i == 0 else jnp.where(lane >= 32 * i, last, high)
        low_ref[12 * u : 12 * u + 12] = low
        high_ref[12 * u : 12 * u + 12] = high
    for index in range(3):
        at = EDGE - 3 * HALO + HALO * index
        low_ref[at : at + HALO] = fields_ref[index, 0:HALO]
        high_ref[at : at + HALO] = fields_ref[index, CY - HALO : CY]


def halves(ref, first, second):
    parts = []
    for at in (first, second):
        rest = ref[pl.ds(at + 8, 4)]
        rest = jnp.concatenate([rest, pltpu.roll(rest, LANES - 16, axis=1)], axis=0)
        parts.append((ref[pl.ds(at, 8)], rest))
    return parts


def unpacked(parts, q):
    lane = lane_of((8, LANES))
    place = lane % 64
    out = None
    for half, (main, rest) in enumerate(parts):
        moved = pltpu.roll(main, (64 * half - 32 * q) % LANES, axis=1)
        tail = pltpu.roll(rest, (64 * half + 32 - 32 * q) % LANES, axis=1)
        moved = jnp.where(place < 32, moved, tail)
        out = moved if out is None else jnp.where(lane < 64, out, moved)
    return jnp.where(place < CHUNK + 2 * HALO, out, 0.0)


def advance(state, south, north, coefs, at):
    west_c, east_c, south_c, north_c, own_c = (ref[at : at + 8] for ref in coefs)
    west = pltpu.roll(state, 1, axis=1)
    east = pltpu.roll(state, LANES - 1, axis=1)
    speed = 0.85 + 0.15 * jnp.tanh(state)
    change = west_c * west + east_c * east
    change = change + (south_c * south + north_c * north)
    return state + speed * (change - own_c * state)


def inside_body(x_ref, fields_ref, mid_ref, steps_ref, seen_ref, total_ref, *coefs):
    fill_coefs(fields_ref[1], fields_ref[2], coefs)
    total_ref[...] = jnp.zeros((CY - 2 * HALO, LANES), jnp.float32)

    def one(index, carry):
        pairs = [index * GROUP + p for p in range(GROUP)]
        for p in pairs:
            parts = halves(x_ref, 12 * p, 12 * (p + PAIRS))
            for q in range(4):
                rows = slice(8 * q, 8 * q + 8)
                out = unpacked(parts, q)
                mid_ref[p, rows] = out
                steps_ref[0, p, rows] = fields_ref[0, rows] + 0.5 * out
        for step in range(NSTEP):
            for q in range(4) if step < NSTEP - 1 else (1, 2):
                at = 8 * q
                for p in pairs:
                    now = steps_ref.at[step, p]
                    state = now[at : at + 8]
                    south = now[at - 1 : at + 7] if q else pltpu.roll(state, 1, axis=0)
                    north = now[at + 1 : at + 9] if q < 3 else pltpu.roll(state, 7, axis=0)
                    state = advance(state, south, north, coefs, at)
                    if step < NSTEP - 1:
                        steps_ref[step + 1, p, at : at + 8] = state
                    else:
                        seen = state + 0.25 * state * state
                        seen_ref[p, at - 8 : at] = seen
                        total_ref[at - 8 : at] += seen
        return carry

    lax.fori_loop(0, PAIRS // GROUP, one, 0)


def cells_body(chunk_ref, value_ref, weight_ref, column_ref, level_ref, out_ref):
    chunk = chunk_ref[0]
    column = column_ref[...]
    row = column // NX
    offset = column % NX - CHUNK * (chunk % 32)
    inside = (offset >= 0) & (offset < CHUNK) & (level_ref[...] == chunk // 32)
    lane = jnp.where(inside, HALO + offset, -1)
    square = weight_ref[...] * weight_ref[...]
    nobs = column.shape[1]
    at_row = lax.broadcasted_iota(jnp.int32, (CY, nobs), 0) == row
    at_lane = (lax.broadcasted_iota(jnp.int32, (LANES, nobs), 0) == lane).astype(jnp.bfloat16)
    parts = []
    for value in (square, square * value_ref[...]):
        left = jnp.where(at_row, value, 0.0)
        for _ in range(3):
            part = left.astype(jnp.bfloat16)
            parts.append(part)
            left = left - part.astype(jnp.float32)
    sums = lax.dot_general(
        jnp.concatenate(parts, axis=0),
        at_lane,
        (((1,), (1,)), ((), ())),
        preferred_element_type=jnp.float32,
    )
    for index in range(2):
        base = 3 * CY * index
        total = sums[base : base + CY] + sums[base + CY : base + 2 * CY]
        total = total + sums[base + 2 * CY : base + 3 * CY]
        out_ref[index] = total


def transport(base, anoms, coefs, buf_ref, first, use):
    for p in range(GROUP):
        at = HALO
        for ref in anoms:
            rows = ref.shape[1]
            buf_ref[0, p, at : at + rows] = base[at - HALO : at - HALO + rows] + 0.5 * ref[first + p]
            at += rows
    for step in range(NSTEP):
        for low in range(0, ROWS, 8) if step < NSTEP - 1 else range(HALO, HALO + CY, 8):
            at = HALO + low
            for p in range(GROUP):
                now = buf_ref.at[step % 2, p]
                state = advance(
                    now[at : at + 8], now[at - 1 : at + 7], now[at + 1 : at + 9], coefs, low
                )
                if step < NSTEP - 1:
                    buf_ref[(step + 1) % 2, p, at : at + 8] = state
                else:
                    use(first + p, low - HALO, state)


def edge_transport(base, low_ref, high_ref, coefs, steps_ref, buf_ref, use):
    for p in range(PAIRS):
        buf_ref[0, p, 0:HALO] = base[0:HALO] + 0.5 * low_ref[p]
        buf_ref[1, p, 2 * HALO : 3 * HALO] = base[HALO + CY :] + 0.5 * high_ref[p]
    for step in range(NSTEP):
        for edge in range(2):
            inside, put, at, low = (
                (step, step + 8, step + 1, step + 1)
                if edge == 0
                else (CY - 8 - step, 8 - step, 15 - step, 39 - step)
            )
            for p in range(PAIRS):
                now = buf_ref.at[edge, p]
                now[put : put + 8] = steps_ref[step, p, inside : inside + 8]
                state = advance(
                    now[at : at + 8], now[at - 1 : at + 7], now[at + 1 : at + 9], coefs, low
                )
                if step < NSTEP - 1:
                    now[at : at + 8] = state
                else:
                    use(p, (CY - HALO) * edge, state)


def blocks(rows):
    return [rows[8 * q : 8 * q + 8] for q in range(4)]


def inner(rows, start):
    lane = lane_of((8, LANES))
    out = None
    for q in range(4):
        moved = pltpu.roll(rows[q], (32 * q - HALO - start) % LANES, axis=1)
        out = moved if out is None else jnp.where(lane >= 32 * q, moved, out)
    return out


def observer(total_ref, obs_ref):
    def use(p, row, state):
        seen = state + 0.25 * state * state
        obs_ref[p, row : row + 8] = seen
        total_ref[row : row + 8] += seen

    return use


def for_groups(work):
    def one(index, carry):
        work(index * GROUP)
        return carry

    lax.fori_loop(0, PAIRS // GROUP, one, 0)


def normal_terms(rows_of, total, cells_ref, gram_ref, dev_ref, left_ref, right_ref):
    center = (total + pltpu.roll(total, 64, axis=1)) * (1.0 / MEMBERS)
    for p in range(PAIRS):
        dev = [rows - center[8 * q : 8 * q + 8] for q, rows in enumerate(rows_of(p))]
        for half in range(2):
            at = 8 * (p + PAIRS * half)
            dev_ref[at : at + 8] = inner(dev, 64 * half)
    weight, weighted = cells_ref[0], cells_ref[1]
    aim = inner(blocks(2.0 * (weighted - weight * center)), 0)
    weight = inner(blocks(4.0 * weight), 0)
    right_ref[MEMBERS:LANES, :] = jnp.zeros((LANES - MEMBERS, 8 * LANES), jnp.float32)
    for r in range(8):
        rows = dev_ref[pl.ds(r, MEMBERS, stride=8), :]
        left_ref[:, LANES * r : LANES * r + LANES] = rows
        right_ref[0:MEMBERS, LANES * r : LANES * r + LANES] = rows * weight[r : r + 1]
        right_ref[MEMBERS : MEMBERS + 1, LANES * r : LANES * r + LANES] = aim[r : r + 1]
    gram = lax.dot_general(
        left_ref[...],
        right_ref[...],
        (((1,), (1,)), ((), ())),
        precision=HIGHEST,
        preferred_element_type=jnp.float32,
    )
    wide = lane_of((MEMBERS, LANES))
    sub = lax.broadcasted_iota(jnp.int32, (MEMBERS, LANES), 0)
    column = jnp.broadcast_to(gram[:, MEMBERS : MEMBERS + 1], (MEMBERS, LANES))
    project = jnp.sum(jnp.where(wide == sub, column, 0.0), axis=0, keepdims=True)
    top, bottom = gram[0:PAIRS], gram[PAIRS:MEMBERS]
    lane, sub = wide[0:PAIRS], sub[0:PAIRS]
    diagonal = jnp.sum(jnp.where(lane - 32 == sub, bottom, 0.0), axis=0, keepdims=True)
    square = jnp.where(lane - 32 >= sub, pltpu.roll(top, 32, axis=1), bottom)
    square = jnp.where(lane < 32, pltpu.roll(top, LANES - 32, axis=1), square)
    packed = jnp.where(lane[0:16] < 64, square[0:16], pltpu.roll(square[16:32], 64, axis=1))
    gram_ref[...] = jnp.zeros((PACKED, LANES), jnp.float32)
    gram_ref[0:8] = packed[0:8]
    gram_ref[8:9] = jnp.where(lane[0:1] < 64, project, pltpu.roll(diagonal, 32, axis=1))
    gram_ref[10:18] = packed[8:16]


def fill_coefs(lon, lat, coefs):
    west_c, east_c, south_c, north_c, own_c = coefs
    west_c[...] = jnp.maximum(lon, 0.0)
    east_c[...] = jnp.maximum(-lon, 0.0)
    south_c[...] = jnp.maximum(lat, 0.0)
    north_c[...] = jnp.maximum(-lat, 0.0)
    own_c[...] = jnp.abs(lon) + jnp.abs(lat)


def first_body(
    low_ref, high_ref, fields_ref, steps_ref, seen_ref, total_ref, cells_ref,
    gram_ref, south_ref, north_ref, full_ref, buf_ref, sum_ref, obs_ref, *scratch
):
    coefs, rest = scratch[:5], scratch[5:]
    for index in range(3):
        at = EDGE - 3 * HALO + HALO * index
        full_ref[index, 0:HALO] = low_ref[at : at + HALO]
        full_ref[index, HALO : HALO + CY] = fields_ref[index]
        full_ref[index, HALO + CY : ROWS] = high_ref[at : at + HALO]
    fill_coefs(full_ref[1], full_ref[2], coefs)
    sum_ref[0:HALO] = jnp.zeros((HALO, LANES), jnp.float32)
    sum_ref[HALO : CY - HALO] = total_ref[...]
    sum_ref[CY - HALO : CY] = jnp.zeros((HALO, LANES), jnp.float32)
    use = observer(sum_ref, obs_ref)
    base = full_ref[0]

    for ref, out_ref in ((low_ref, south_ref), (high_ref, north_ref)):
        for u in range(PAIRS // 4):
            parts = halves(ref, 12 * u, 12 * (u + PAIRS // 4))
            for i in range(4):
                out_ref[4 * u + i] = unpacked(parts, i)
    edge_transport(base, south_ref, north_ref, coefs, steps_ref, buf_ref, use)

    def rows_of(p):
        return [obs_ref[p, 0:8], seen_ref[p, 0:8], seen_ref[p, 8:16], obs_ref[p, 24:32]]

    normal_terms(rows_of, sum_ref[...], cells_ref, gram_ref, *rest)


def solve(core, own, other, weights):
    shape = (MEMBERS, LANES)
    wide = lane_of(shape)
    sub = lax.broadcasted_iota(jnp.int32, shape, 0)
    left = MEMBERS - 1.0
    low, high = jnp.where(core == 0, own, other), jnp.where(core == 0, other, own)
    packed = jnp.concatenate([low[0:8], high[0:8]], axis=0)
    ends = jnp.broadcast_to(low[8:9], shape)
    square = jnp.concatenate([packed, pltpu.roll(packed, 64, axis=1)], axis=0)
    padded = jnp.concatenate([square, jnp.zeros((LANES - PAIRS, LANES), jnp.float32)], axis=0)
    turned = jnp.transpose(padded)
    lane, row = wide[0:PAIRS], sub[0:PAIRS]
    top = jnp.where(lane >= row, pltpu.roll(square, LANES - 32, axis=1), turned[32:64])
    top = jnp.where(lane < 32, top, pltpu.roll(square, 32, axis=1))
    bottom = jnp.where(lane - 32 < row, square, pltpu.roll(turned[32:64], 32, axis=1))
    bottom = jnp.where(lane - 32 == row, pltpu.roll(ends, LANES - 32, axis=1)[0:PAIRS], bottom)
    bottom = jnp.where(lane < 32, turned[0:32], bottom)
    sums = jnp.concatenate([top, bottom], axis=0)
    project = jnp.sum(jnp.where(wide == sub, ends, 0.0), axis=1, keepdims=True)
    gradient = left * weights - jnp.broadcast_to(project, shape)
    lane = wide
    matrix = jnp.where(
        lane < MEMBERS,
        sums + jnp.where(lane == sub, left, 0.0),
        jnp.where(lane == MEMBERS, gradient, 0.0),
    )
    width = 8
    for start in range(0, MEMBERS, width):
        columns = [
            jnp.broadcast_to(matrix[:, start + j : start + j + 1], shape) for j in range(width)
        ]
        for j in range(width):
            k = start + j
            factor = jnp.where(sub == k, 0.0, columns[j] * (1.0 / columns[j][k : k + 1]))
            for later in range(j + 1, width):
                columns[later] = columns[later] - factor * columns[later][k : k + 1]
            matrix = matrix - factor * matrix[k : k + 1]
    diagonal = jnp.sum(jnp.where(lane == sub, matrix, 0.0), axis=1, keepdims=True)
    solved = matrix[:, MEMBERS : MEMBERS + 1] / diagonal
    return weights - jnp.broadcast_to(solved, shape)


def by_pair(weights):
    lane = lane_of((PAIRS, LANES))
    return jnp.where(lane < 64, weights[0:PAIRS], weights[PAIRS:MEMBERS])


def mix(pair_ref, anoms_ref):
    total = jnp.zeros(anoms_ref.shape[1:], jnp.float32)
    for p in range(PAIRS):
        total = total + pair_ref[p : p + 1] * anoms_ref[p]
    return total + pltpu.roll(total, 64, axis=1)


def second_body(
    core_ref, own_ref, other_ref, south_ref, mid_ref, north_ref, full_ref, cells_ref,
    gram_ref, weights_ref, pair_ref, buf_ref, sum_ref, obs_ref, *scratch
):
    coefs, rest = scratch[:5], scratch[5:]
    fill_coefs(full_ref[1], full_ref[2], coefs)
    weights = solve(
        core_ref[0], own_ref[...], other_ref[...], jnp.zeros((MEMBERS, LANES), jnp.float32)
    )
    weights_ref[...] = weights
    pair_ref[...] = by_pair(weights)
    anoms = (south_ref, mid_ref, north_ref)
    base = full_ref[0] + jnp.concatenate([mix(pair_ref, ref) for ref in anoms], axis=0)
    edge = jnp.zeros((2, GROUP, HALO, LANES), jnp.float32)
    buf_ref[:, :, 0:HALO] = edge
    buf_ref[:, :, HALO + ROWS :] = edge
    sum_ref[...] = jnp.zeros((CY, LANES), jnp.float32)
    use = observer(sum_ref, obs_ref)
    for_groups(lambda first: transport(base, anoms, coefs, buf_ref, first, use))
    normal_terms(
        lambda p: blocks(obs_ref[p]), sum_ref[...], cells_ref, gram_ref, *rest
    )


def last_body(core_ref, own_ref, other_ref, weights_ref, mid_ref, out_ref, pair_ref):
    weights = solve(core_ref[0], own_ref[...], other_ref[...], weights_ref[...])
    pair_ref[...] = by_pair(weights)
    out_ref[...] = inner(blocks(mix(pair_ref, mid_ref)), 0)


def spread_body(core_ref, own_ref, other_ref, out_ref):
    lane = lane_of((8, LANES))
    first = core_ref[0] == 0
    for lev in range(LEV):
        for b in range(8):
            pieces = []
            for k in range(4):
                at = 16 * lev + 2 * b + k // 2
                own, other = own_ref[at], other_ref[at]
                if k % 2:
                    own, other = other, own
                pieces.append(jnp.where(first, own, other))
            for q in range(4):
                out = None
                for k in range(4):
                    moved = pltpu.roll(pieces[k], (32 * (k - q)) % LANES, axis=1)
                    out = moved if out is None else jnp.where(lane >= 32 * k, moved, out)
                out_ref[lev, 8 * q : 8 * q + 8, LANES * b : LANES * b + LANES] = out


def exchange(array, axes):
    return lax.all_to_all(array, axes, 0, 0, tiled=True)


def to_all(array, axes, count):
    return exchange(jnp.broadcast_to(array[None], (count, *array.shape)), axes)


def swap_cores(array):
    return lax.ppermute(array, "core", [(0, 1), (1, 0)])


def sum_everywhere(packed):
    shape = (5, 2, LANES)
    halves = jnp.broadcast_to(packed.reshape(1, 2, 1, *shape), (2, 2, 8, *shape))
    part = jnp.sum(exchange(halves.reshape(32, *shape), PLANE), axis=0)
    part = jnp.sum(to_all(part, "z", 16), axis=0).reshape(10, LANES)
    return part, swap_cores(part)


def local(
    background, anomalies, courant_lon, courant_lat, obs_value, obs_weight, obs_column, obs_level
):
    chunk = lax.axis_index(MEM).astype(jnp.int32).reshape(1)
    core = lax.axis_index("core").astype(jnp.int32).reshape(1)
    pieces = call(pack_body, f32(MEMBERS * 12, LANES), in_specs=[VMEM])(anomalies[0])
    pieces = exchange(pieces.reshape(MEMBERS, 3, 4, LANES), MEM).reshape(MEMBERS * 12, LANES)
    nobs = obs_value.shape[0]
    flat = [a.reshape(1, nobs) for a in (obs_value, obs_weight, obs_column, obs_level)]
    cells = call(cells_body, f32(2, CY, LANES), in_specs=[SMEM] + [VMEM] * 4)(chunk, *flat)
    fields = call(fields_body, f32(3, CY, LANES), in_specs=[SMEM] + [VMEM] * 3)(
        chunk, background, courant_lon, courant_lat
    )
    pieces, fields, cells = lax.optimization_barrier((pieces, fields, cells))
    low_edge, high_edge = call(
        edges_body, (f32(EDGE, LANES), f32(EDGE, LANES)), in_specs=[VMEM] * 2
    )(pieces, fields)
    forward = [(i, i + 1) for i in range(7)]
    backward = [(i + 1, i) for i in range(7)]
    low = lax.ppermute(high_edge, TILE, forward)
    high = lax.ppermute(low_edge, TILE, backward)
    mid, steps, seen, total = call(
        inside_body,
        (
            f32(PAIRS, CY, LANES),
            f32(NSTEP, PAIRS, CY, LANES),
            f32(PAIRS, CY - 2 * HALO, LANES),
            f32(CY - 2 * HALO, LANES),
        ),
        [pltpu.VMEM((CY, LANES), jnp.float32)] * 5,
        in_specs=[VMEM] * 2,
    )(pieces, fields)
    rest = [
        pltpu.VMEM((CY, LANES), jnp.float32),
        pltpu.VMEM((PAIRS, CY, LANES), jnp.float32),
        *[pltpu.VMEM((ROWS, LANES), jnp.float32)] * 5,
        pltpu.VMEM((MEMBERS * 8, LANES), jnp.float32),
        pltpu.VMEM((MEMBERS, 8 * LANES), jnp.float32),
        pltpu.VMEM((LANES, 8 * LANES), jnp.float32),
    ]
    pair = pltpu.VMEM((PAIRS, LANES), jnp.float32)
    gram, south, north, full = call(
        first_body,
        (f32(PACKED, LANES), *[f32(PAIRS, HALO, LANES)] * 2, f32(3, ROWS, LANES)),
        [pltpu.VMEM((2, PAIRS, 3 * HALO, LANES), jnp.float32), *rest],
        in_specs=[VMEM] * 7,
    )(low, high, fields, steps, seen, total, cells)
    gram, weights = call(
        second_body,
        (f32(PACKED, LANES), f32(MEMBERS, LANES)),
        [pair, pltpu.VMEM((2, GROUP, ROWS + 2 * HALO, LANES), jnp.float32), *rest],
        in_specs=[SMEM] + [VMEM] * 7,
    )(core, *sum_everywhere(gram), south, mid, north, full, cells)
    part = call(last_body, f32(8, LANES), [pair], in_specs=[SMEM] + [VMEM] * 4)(
        core, *sum_everywhere(gram), weights, mid
    )
    parts = to_all(part, ("z", "yl"), 32)
    return call(spread_body, f32(LEV, CY, NX), in_specs=[SMEM] + [VMEM] * 2)(
        core, parts, swap_cores(parts)
    )


def solution(mesh):
    fine = Mesh(mesh.devices.reshape(16, 2, 2, 2, 4), ("z", "yl", "core", "yh", "x"))
    return jax.shard_map(
        local,
        mesh=fine,
        in_specs=(
            P(None, TILE, None),
            P(MEM, None, TILE, None),
            P(None, TILE, None),
            P(None, TILE, None),
            P(TILE),
            P(TILE),
            P(TILE),
            P(TILE),
        ),
        out_specs=P(None, TILE, None),
        check_vma=False,
    )
```

```python
import functools

import jax
import jax.numpy as jnp
from jax import lax
from jax.experimental import pallas as pl
from jax.experimental.pallas import tpu as pltpu
from jax.sharding import Mesh, PartitionSpec as P

NSTEP = 8
MEMBERS = 64
PAIRS = 32
GROUP = 8
LEV = 2
CY = 32
NX = 1024
CHUNK = 32
HALO = 8
ROWS = CY + 2 * HALO
EDGE = 12 * MEMBERS // 4 + 3 * HALO
LANES = 128
PACKED = 20
HIGHEST = lax.Precision.HIGHEST

MEM = ("z", "yl", "core")
TILE = ("yh", "x")
PLANE = ("yl", "core", "yh", "x")
VMEM = pl.BlockSpec(memory_space=pltpu.VMEM)
SMEM = pl.BlockSpec(memory_space=pltpu.SMEM)


def lane_of(shape):
    return lax.broadcasted_iota(jnp.int32, shape, len(shape) - 1)


def call(body, out, scratch=(), in_specs=None, vmem=40 << 20):
    return pl.pallas_call(
        body,
        out_shape=out,
        in_specs=in_specs,
        out_specs=jax.tree.map(lambda _: VMEM, out),
        scratch_shapes=list(scratch),
        compiler_params=pltpu.CompilerParams(vmem_limit_bytes=vmem),
    )


def f32(*shape):
    return jax.ShapeDtypeStruct(shape, jnp.float32)


def pack_body(own_ref, pieces_ref):
    lane = lane_of((8, LANES))
    for lev in range(LEV):
        turned = []
        for q in range(4):
            rolled = [
                pltpu.roll(own_ref[lev, 8 * q : 8 * q + 8, LANES * b : LANES * b + LANES], HALO, axis=1)
                for b in range(8)
            ]
            shifted = [jnp.where(lane < HALO, rolled[b - 1], rolled[b]) for b in range(8)]
            turned.append(
                [
                    [pltpu.roll(block, 32 * n, axis=1) if n else block for n in range(4)]
                    for block in shifted
                ]
            )

        def gather(b, k):
            out = turned[0][b][(-k) % 4]
            for q in range(1, 4):
                out = jnp.where(lane >= 32 * q, turned[q][b][(q - k) % 4], out)
            return out

        for b in range(8):
            for k in range(4):
                at = 12 * (32 * lev + 4 * b + k)
                pieces_ref[at + 4 : at + 12] = gather(b, k)
                rest = gather(b, k + 1) if k < 3 else gather((b + 1) % 8, 0)
                other = pltpu.roll(rest, 16, axis=1)
                pieces_ref[at : at + 4] = jnp.where(
                    lane[0:4] % 32 < 16, rest[0:4], other[4:8]
                )


def fields_body(chunk_ref, bg_ref, lon_ref, lat_ref, fields_ref):
    chunk = chunk_ref[0]
    lev, b, k = chunk // 32, chunk % 32 // 4, chunk % 4
    wide = lane_of((CY, LANES))

    def block(ref, index):
        return ref[lev, :, pl.ds(pl.multiple_of(index * LANES, LANES), LANES)]

    for index, ref in enumerate((bg_ref, lon_ref, lat_ref)):
        mid = block(ref, b)
        mid = jnp.where((wide >= LANES - HALO) & (k == 0), block(ref, (b + 7) % 8), mid)
        mid = jnp.where((wide < HALO) & (k == 3), block(ref, (b + 1) % 8), mid)
        mid = pltpu.roll(mid, (HALO - CHUNK * k + LANES) % LANES, axis=1)
        mid = jnp.where(wide < CHUNK + 2 * HALO, mid, 0.0)
        fields_ref[index] = jnp.where(wide < 64, mid, pltpu.roll(mid, 64, axis=1))


def edges_body(x_ref, fields_ref, low_ref, high_ref):
    for u in range(MEMBERS // 4):
        for row, count in ((0, 4), (4, 8)):
            lane = lane_of((count, LANES))
            low, high = None, None
            for i in range(4):
                at = 12 * (4 * u + i) + row
                piece = x_ref[at : at + count]
                first = pltpu.roll(piece, 32 * i, axis=1) if i else piece
                last = pltpu.roll(piece, (32 * i + 32) % LANES, axis=1) if i < 3 else piece
                low = first if i == 0 else jnp.where(lane >= 32 * i, first, low)
                high = last if i == 0 else jnp.where(lane >= 32 * i, last, high)
            at = 12 * u + row
            low_ref[at : at + count] = low
            high_ref[at : at + count] = high
    for index in range(3):
        at = EDGE - 3 * HALO + HALO * index
        low_ref[at : at + HALO] = fields_ref[index, 0:HALO]
        high_ref[at : at + HALO] = fields_ref[index, CY - HALO : CY]


def halves(ref, first, second):
    parts = []
    for at in (first, second):
        rest = ref[pl.ds(at, 4)]
        rest = jnp.concatenate([rest, pltpu.roll(rest, LANES - 16, axis=1)], axis=0)
        parts.append((ref[pl.ds(at + 4, 8)], rest))
    return parts


def unpacked(parts, q):
    lane = lane_of((8, LANES))
    place = lane % 64
    out = None
    for half, (main, rest) in enumerate(parts):
        moved = pltpu.roll(main, (64 * half - 32 * q) % LANES, axis=1)
        tail = pltpu.roll(rest, (64 * half + 32 - 32 * q) % LANES, axis=1)
        moved = jnp.where(place < 32, moved, tail)
        out = moved if out is None else jnp.where(lane < 64, out, moved)
    return jnp.where(place < CHUNK + 2 * HALO, out, 0.0)


def advance(state, south, north, coefs, at):
    west_c, east_c, south_c, north_c, own_c = (ref[at : at + 8] for ref in coefs)
    west = pltpu.roll(state, 1, axis=1)
    east = pltpu.roll(state, LANES - 1, axis=1)
    speed = 0.85 + 0.15 * jnp.tanh(state)
    change = west_c * west + east_c * east
    change = change + (south_c * south + north_c * north)
    return state + speed * (change - own_c * state)


def inside_body(x_ref, fields_ref, mid_ref, steps_ref, seen_ref, total_ref, *coefs):
    fill_coefs(fields_ref[1], fields_ref[2], coefs)
    total_ref[...] = jnp.zeros((CY - 2 * HALO, LANES), jnp.float32)

    def one(index, carry):
        pairs = [index * GROUP + p for p in range(GROUP)]
        for p in pairs:
            parts = halves(x_ref, 12 * p, 12 * (p + PAIRS))
            for q in range(4):
                rows = slice(8 * q, 8 * q + 8)
                out = unpacked(parts, q)
                mid_ref[p, rows] = out
                steps_ref[0, p, rows] = fields_ref[0, rows] + 0.5 * out
        for step in range(NSTEP):
            for q in range(4) if step < NSTEP - 1 else (1, 2):
                at = 8 * q
                for p in pairs:
                    now = steps_ref.at[step, p]
                    state = now[at : at + 8]
                    south = now[at - 1 : at + 7] if q else pltpu.roll(state, 1, axis=0)
                    north = now[at + 1 : at + 9] if q < 3 else pltpu.roll(state, 7, axis=0)
                    state = advance(state, south, north, coefs, at)
                    if step < NSTEP - 1:
                        steps_ref[step + 1, p, at : at + 8] = state
                    else:
                        seen = state + 0.25 * state * state
                        seen_ref[p, at - 8 : at] = seen
                        total_ref[at - 8 : at] += seen
        return carry

    lax.fori_loop(0, PAIRS // GROUP, one, 0)


def cells_body(chunk_ref, value_ref, weight_ref, column_ref, level_ref, out_ref):
    chunk = chunk_ref[0]
    column = column_ref[...]
    row = column // NX
    offset = column % NX - CHUNK * (chunk % 32)
    inside = (offset >= 0) & (offset < CHUNK) & (level_ref[...] == chunk // 32)
    lane = jnp.where(inside, HALO + offset, -1)
    square = weight_ref[...] * weight_ref[...]
    nobs = column.shape[1]
    at_row = lax.broadcasted_iota(jnp.int32, (CY, nobs), 0) == row
    at_lane = (lax.broadcasted_iota(jnp.int32, (LANES, nobs), 0) == lane).astype(jnp.bfloat16)
    parts = []
    for value in (square, square * value_ref[...]):
        left = jnp.where(at_row, value, 0.0)
        for _ in range(3):
            part = left.astype(jnp.bfloat16)
            parts.append(part)
            left = left - part.astype(jnp.float32)
    sums = lax.dot_general(
        jnp.concatenate(parts, axis=0),
        at_lane,
        (((1,), (1,)), ((), ())),
        preferred_element_type=jnp.float32,
    )
    for index in range(2):
        base = 3 * CY * index
        total = sums[base : base + CY] + sums[base + CY : base + 2 * CY]
        total = total + sums[base + 2 * CY : base + 3 * CY]
        out_ref[index] = total


def transport(base, anoms, coefs, buf_ref, first, use):
    for p in range(GROUP):
        at = HALO
        for ref in anoms:
            rows = ref.shape[1]
            buf_ref[0, p, at : at + rows] = base[at - HALO : at - HALO + rows] + 0.5 * ref[first + p]
            at += rows
    for step in range(NSTEP):
        for low in range(0, ROWS, 8) if step < NSTEP - 1 else range(HALO, HALO + CY, 8):
            at = HALO + low
            for p in range(GROUP):
                now = buf_ref.at[step % 2, p]
                state = advance(
                    now[at : at + 8], now[at - 1 : at + 7], now[at + 1 : at + 9], coefs, low
                )
                if step < NSTEP - 1:
                    buf_ref[(step + 1) % 2, p, at : at + 8] = state
                else:
                    use(first + p, low - HALO, state)


def edge_transport(base, low_ref, high_ref, coefs, steps_ref, buf_ref, use):
    for p in range(PAIRS):
        buf_ref[0, p, 0:HALO] = base[0:HALO] + 0.5 * low_ref[p]
        buf_ref[1, p, 2 * HALO : 3 * HALO] = base[HALO + CY :] + 0.5 * high_ref[p]
    for step in range(NSTEP):
        for edge in range(2):
            inside, put, at, low = (
                (step, step + 8, step + 1, step + 1)
                if edge == 0
                else (CY - 8 - step, 8 - step, 15 - step, 39 - step)
            )
            for p in range(PAIRS):
                now = buf_ref.at[edge, p]
                now[put : put + 8] = steps_ref[step, p, inside : inside + 8]
                state = advance(
                    now[at : at + 8], now[at - 1 : at + 7], now[at + 1 : at + 9], coefs, low
                )
                if step < NSTEP - 1:
                    now[at : at + 8] = state
                else:
                    use(p, (CY - HALO) * edge, state)


def blocks(rows):
    return [rows[8 * q : 8 * q + 8] for q in range(4)]


def inner(rows, start):
    lane = lane_of((8, LANES))
    out = None
    for q in range(4):
        moved = pltpu.roll(rows[q], (32 * q - HALO - start) % LANES, axis=1)
        out = moved if out is None else jnp.where(lane >= 32 * q, moved, out)
    return out


def observer(total_ref, obs_ref):
    def use(p, row, state):
        seen = state + 0.25 * state * state
        obs_ref[p, row : row + 8] = seen
        total_ref[row : row + 8] += seen

    return use


def for_groups(work):
    def one(index, carry):
        work(index * GROUP)
        return carry

    lax.fori_loop(0, PAIRS // GROUP, one, 0)


def normal_terms(rows_of, total, cells_ref, gram_ref, dev_ref, left_ref, right_ref):
    center = (total + pltpu.roll(total, 64, axis=1)) * (1.0 / MEMBERS)
    for p in range(PAIRS):
        dev = [rows - center[8 * q : 8 * q + 8] for q, rows in enumerate(rows_of(p))]
        for half in range(2):
            at = 8 * (p + PAIRS * half)
            dev_ref[at : at + 8] = inner(dev, 64 * half)
    weight, weighted = cells_ref[0], cells_ref[1]
    aim = inner(blocks(2.0 * (weighted - weight * center)), 0)
    weight = inner(blocks(4.0 * weight), 0)
    right_ref[MEMBERS:LANES, :] = jnp.zeros((LANES - MEMBERS, 8 * LANES), jnp.float32)
    for r in range(8):
        rows = dev_ref[pl.ds(r, MEMBERS, stride=8), :]
        left_ref[:, LANES * r : LANES * r + LANES] = rows
        right_ref[0:MEMBERS, LANES * r : LANES * r + LANES] = rows * weight[r : r + 1]
        right_ref[MEMBERS : MEMBERS + 1, LANES * r : LANES * r + LANES] = aim[r : r + 1]
    gram = lax.dot_general(
        left_ref[...],
        right_ref[...],
        (((1,), (1,)), ((), ())),
        precision=HIGHEST,
        preferred_element_type=jnp.float32,
    )
    wide = lane_of((MEMBERS, LANES))
    sub = lax.broadcasted_iota(jnp.int32, (MEMBERS, LANES), 0)
    column = jnp.broadcast_to(gram[:, MEMBERS : MEMBERS + 1], (MEMBERS, LANES))
    project = jnp.sum(jnp.where(wide == sub, column, 0.0), axis=0, keepdims=True)
    top, bottom = gram[0:PAIRS], gram[PAIRS:MEMBERS]
    lane, sub = wide[0:PAIRS], sub[0:PAIRS]
    diagonal = jnp.sum(jnp.where(lane - 32 == sub, bottom, 0.0), axis=0, keepdims=True)
    square = jnp.where(lane - 32 >= sub, pltpu.roll(top, 32, axis=1), bottom)
    square = jnp.where(lane < 32, pltpu.roll(top, LANES - 32, axis=1), square)
    packed = jnp.where(lane[0:16] < 64, square[0:16], pltpu.roll(square[16:32], 64, axis=1))
    gram_ref[...] = jnp.zeros((PACKED, LANES), jnp.float32)
    gram_ref[0:8] = packed[0:8]
    gram_ref[8:9] = jnp.where(lane[0:1] < 64, project, pltpu.roll(diagonal, 32, axis=1))
    gram_ref[10:18] = packed[8:16]


def fill_coefs(lon, lat, coefs):
    west_c, east_c, south_c, north_c, own_c = coefs
    west_c[...] = jnp.maximum(lon, 0.0)
    east_c[...] = jnp.maximum(-lon, 0.0)
    south_c[...] = jnp.maximum(lat, 0.0)
    north_c[...] = jnp.maximum(-lat, 0.0)
    own_c[...] = jnp.abs(lon) + jnp.abs(lat)


def first_body(
    low_ref, high_ref, fields_ref, steps_ref, seen_ref, total_ref, cells_ref,
    gram_ref, south_ref, north_ref, full_ref, buf_ref, sum_ref, obs_ref, *scratch
):
    coefs, rest = scratch[:5], scratch[5:]
    for index in range(3):
        at = EDGE - 3 * HALO + HALO * index
        full_ref[index, 0:HALO] = low_ref[at : at + HALO]
        full_ref[index, HALO : HALO + CY] = fields_ref[index]
        full_ref[index, HALO + CY : ROWS] = high_ref[at : at + HALO]
    fill_coefs(full_ref[1], full_ref[2], coefs)
    sum_ref[0:HALO] = jnp.zeros((HALO, LANES), jnp.float32)
    sum_ref[HALO : CY - HALO] = total_ref[...]
    sum_ref[CY - HALO : CY] = jnp.zeros((HALO, LANES), jnp.float32)
    use = observer(sum_ref, obs_ref)
    base = full_ref[0]

    for ref, out_ref in ((low_ref, south_ref), (high_ref, north_ref)):
        for u in range(PAIRS // 4):
            parts = halves(ref, 12 * u, 12 * (u + PAIRS // 4))
            for i in range(4):
                out_ref[4 * u + i] = unpacked(parts, i)
    edge_transport(base, south_ref, north_ref, coefs, steps_ref, buf_ref, use)

    def rows_of(p):
        return [obs_ref[p, 0:8], seen_ref[p, 0:8], seen_ref[p, 8:16], obs_ref[p, 24:32]]

    normal_terms(rows_of, sum_ref[...], cells_ref, gram_ref, *rest)


def solve(packed, weights):
    shape = (MEMBERS, LANES)
    wide = lane_of(shape)
    sub = lax.broadcasted_iota(jnp.int32, shape, 0)
    left = MEMBERS - 1.0
    low, high = packed[0], packed[1]
    packed = jnp.concatenate([low[0:8], high[0:8]], axis=0)
    ends = jnp.broadcast_to(low[8:9], shape)
    square = jnp.concatenate([packed, pltpu.roll(packed, 64, axis=1)], axis=0)
    padded = jnp.concatenate([square, jnp.zeros((LANES - PAIRS, LANES), jnp.float32)], axis=0)
    turned = jnp.transpose(padded)
    lane, row = wide[0:PAIRS], sub[0:PAIRS]
    top = jnp.where(lane >= row, pltpu.roll(square, LANES - 32, axis=1), turned[32:64])
    top = jnp.where(lane < 32, top, pltpu.roll(square, 32, axis=1))
    bottom = jnp.where(lane - 32 < row, square, pltpu.roll(turned[32:64], 32, axis=1))
    bottom = jnp.where(lane - 32 == row, pltpu.roll(ends, LANES - 32, axis=1)[0:PAIRS], bottom)
    bottom = jnp.where(lane < 32, turned[0:32], bottom)
    sums = jnp.concatenate([top, bottom], axis=0)
    project = jnp.sum(jnp.where(wide == sub, ends, 0.0), axis=1, keepdims=True)
    gradient = left * weights - jnp.broadcast_to(project, shape)
    lane = wide
    matrix = jnp.where(
        lane < MEMBERS,
        sums + jnp.where(lane == sub, left, 0.0),
        jnp.where(lane == MEMBERS, gradient, 0.0),
    )
    width = 8
    for start in range(0, MEMBERS, width):
        columns = [
            jnp.broadcast_to(matrix[:, start + j : start + j + 1], shape) for j in range(width)
        ]
        for j in range(width):
            k = start + j
            factor = jnp.where(sub == k, 0.0, columns[j] * (1.0 / columns[j][k : k + 1]))
            for later in range(j + 1, width):
                columns[later] = columns[later] - factor * columns[later][k : k + 1]
            matrix = matrix - factor * matrix[k : k + 1]
    diagonal = jnp.sum(jnp.where(lane == sub, matrix, 0.0), axis=1, keepdims=True)
    solved = matrix[:, MEMBERS : MEMBERS + 1] / diagonal
    return weights - jnp.broadcast_to(solved, shape)


def by_pair(weights):
    lane = lane_of((PAIRS, LANES))
    return jnp.where(lane < 64, weights[0:PAIRS], weights[PAIRS:MEMBERS])


def mix(pair_ref, anoms_ref):
    total = jnp.zeros(anoms_ref.shape[1:], jnp.float32)
    for p in range(PAIRS):
        total = total + pair_ref[p : p + 1] * anoms_ref[p]
    return total + pltpu.roll(total, 64, axis=1)


def second_body(
    sums_ref, south_ref, mid_ref, north_ref, full_ref, cells_ref,
    gram_ref, weights_ref, pair_ref, buf_ref, sum_ref, obs_ref, *scratch
):
    coefs, rest = scratch[:5], scratch[5:]
    fill_coefs(full_ref[1], full_ref[2], coefs)
    weights = solve(sums_ref[...], jnp.zeros((MEMBERS, LANES), jnp.float32))
    weights_ref[...] = weights
    pair_ref[...] = by_pair(weights)
    anoms = (south_ref, mid_ref, north_ref)
    base = full_ref[0] + jnp.concatenate([mix(pair_ref, ref) for ref in anoms], axis=0)
    edge = jnp.zeros((2, GROUP, HALO, LANES), jnp.float32)
    buf_ref[:, :, 0:HALO] = edge
    buf_ref[:, :, HALO + ROWS :] = edge
    sum_ref[...] = jnp.zeros((CY, LANES), jnp.float32)
    use = observer(sum_ref, obs_ref)
    for_groups(lambda first: transport(base, anoms, coefs, buf_ref, first, use))
    normal_terms(
        lambda p: blocks(obs_ref[p]), sum_ref[...], cells_ref, gram_ref, *rest
    )


def last_body(sums_ref, weights_ref, mid_ref, out_ref, pair_ref):
    weights = solve(sums_ref[...], weights_ref[...])
    pair_ref[...] = by_pair(weights)
    out_ref[...] = inner(blocks(mix(pair_ref, mid_ref)), 0)


def spread_body(pieces_ref, out_ref):
    lane = lane_of((8, LANES))
    for lev in range(LEV):
        for b in range(8):
            pieces = [pieces_ref[k % 2, 16 * lev + 2 * b + k // 2] for k in range(4)]
            for q in range(4):
                out = None
                for k in range(4):
                    moved = pltpu.roll(pieces[k], (32 * (k - q)) % LANES, axis=1)
                    out = moved if out is None else jnp.where(lane >= 32 * k, moved, out)
                out_ref[lev, 8 * q : 8 * q + 8, LANES * b : LANES * b + LANES] = out


def exchange(array, axes):
    return lax.all_to_all(array, axes, 0, 0, tiled=True)


def to_all(array, axes, count):
    return exchange(jnp.broadcast_to(array[None], (count, *array.shape)), axes)


def both_cores(array):
    return lax.all_gather(array, "core")


def sum_everywhere(packed):
    shape = (5, 2, LANES)
    halves = jnp.broadcast_to(packed.reshape(1, 2, 1, *shape), (2, 2, 8, *shape))
    part = jnp.sum(exchange(halves.reshape(32, *shape), PLANE), axis=0)
    part = jnp.sum(to_all(part, "z", 16), axis=0).reshape(10, LANES)
    return both_cores(part)


def local(
    background, anomalies, courant_lon, courant_lat, obs_value, obs_weight, obs_column, obs_level
):
    chunk = lax.axis_index(MEM).astype(jnp.int32).reshape(1)
    pieces = call(pack_body, f32(MEMBERS * 12, LANES), in_specs=[VMEM])(anomalies[0])
    pieces = exchange(pieces.reshape(MEMBERS, 3, 4, LANES), MEM).reshape(MEMBERS * 12, LANES)
    nobs = obs_value.shape[0]
    flat = [a.reshape(1, nobs) for a in (obs_value, obs_weight, obs_column, obs_level)]
    cells = call(cells_body, f32(2, CY, LANES), in_specs=[SMEM] + [VMEM] * 4)(chunk, *flat)
    fields = call(fields_body, f32(3, CY, LANES), in_specs=[SMEM] + [VMEM] * 3)(
        chunk, background, courant_lon, courant_lat
    )
    pieces, fields, cells = lax.optimization_barrier((pieces, fields, cells))
    low_edge, high_edge = call(
        edges_body, (f32(EDGE, LANES), f32(EDGE, LANES)), in_specs=[VMEM] * 2
    )(pieces, fields)
    forward = [(i, i + 1) for i in range(7)]
    backward = [(i + 1, i) for i in range(7)]
    low = lax.ppermute(high_edge, TILE, forward)
    high = lax.ppermute(low_edge, TILE, backward)
    mid, steps, seen, total = call(
        inside_body,
        (
            f32(PAIRS, CY, LANES),
            f32(NSTEP, PAIRS, CY, LANES),
            f32(PAIRS, CY - 2 * HALO, LANES),
            f32(CY - 2 * HALO, LANES),
        ),
        [pltpu.VMEM((CY, LANES), jnp.float32)] * 5,
        in_specs=[VMEM] * 2,
    )(pieces, fields)
    rest = [
        pltpu.VMEM((CY, LANES), jnp.float32),
        pltpu.VMEM((PAIRS, CY, LANES), jnp.float32),
        *[pltpu.VMEM((ROWS, LANES), jnp.float32)] * 5,
        pltpu.VMEM((MEMBERS * 8, LANES), jnp.float32),
        pltpu.VMEM((MEMBERS, 8 * LANES), jnp.float32),
        pltpu.VMEM((LANES, 8 * LANES), jnp.float32),
    ]
    pair = pltpu.VMEM((PAIRS, LANES), jnp.float32)
    gram, south, north, full = call(
        first_body,
        (f32(PACKED, LANES), *[f32(PAIRS, HALO, LANES)] * 2, f32(3, ROWS, LANES)),
        [pltpu.VMEM((2, PAIRS, 3 * HALO, LANES), jnp.float32), *rest],
        in_specs=[VMEM] * 7,
    )(low, high, fields, steps, seen, total, cells)
    gram, weights = call(
        second_body,
        (f32(PACKED, LANES), f32(MEMBERS, LANES)),
        [pair, pltpu.VMEM((2, GROUP, ROWS + 2 * HALO, LANES), jnp.float32), *rest],
        in_specs=[VMEM] * 6,
    )(sum_everywhere(gram), south, mid, north, full, cells)
    part = call(last_body, f32(8, LANES), [pair], in_specs=[VMEM] * 3)(
        sum_everywhere(gram), weights, mid
    )
    parts = both_cores(to_all(part, ("z", "yl"), 32))
    return call(spread_body, f32(LEV, CY, NX), in_specs=[VMEM])(parts)


def solution(mesh):
    fine = Mesh(mesh.devices.reshape(16, 2, 2, 2, 4), ("z", "yl", "core", "yh", "x"))
    return jax.shard_map(
        local,
        mesh=fine,
        in_specs=(
            P(None, TILE, None),
            P(MEM, None, TILE, None),
            P(None, TILE, None),
            P(None, TILE, None),
            P(TILE),
            P(TILE),
            P(TILE),
            P(TILE),
        ),
        out_specs=P(None, TILE, None),
        check_vma=False,
    )
```

```python
import functools

import jax
import jax.numpy as jnp
from jax import lax
from jax.experimental import pallas as pl
from jax.experimental.pallas import tpu as pltpu
from jax.sharding import Mesh, PartitionSpec as P

NSTEP = 8
MEMBERS = 64
PAIRS = 32
GROUP = 16
LEV = 2
CY = 32
NX = 1024
CHUNK = 32
HALO = 8
ROWS = CY + 2 * HALO
EDGE = 12 * MEMBERS // 4 + 3 * HALO
LANES = 128
PACKED = 20
HIGHEST = lax.Precision.HIGHEST

MEM = ("z", "yl", "core")
TILE = ("yh", "x")
PLANE = ("yl", "core", "yh", "x")
VMEM = pl.BlockSpec(memory_space=pltpu.VMEM)
SMEM = pl.BlockSpec(memory_space=pltpu.SMEM)


def lane_of(shape):
    return lax.broadcasted_iota(jnp.int32, shape, len(shape) - 1)


def call(body, out, scratch=(), in_specs=None, vmem=40 << 20):
    return pl.pallas_call(
        body,
        out_shape=out,
        in_specs=in_specs,
        out_specs=jax.tree.map(lambda _: VMEM, out),
        scratch_shapes=list(scratch),
        compiler_params=pltpu.CompilerParams(vmem_limit_bytes=vmem),
    )


def f32(*shape):
    return jax.ShapeDtypeStruct(shape, jnp.float32)


def pack_body(own_ref, pieces_ref):
    lane = lane_of((8, LANES))
    for lev in range(LEV):
        turned = []
        for q in range(4):
            rolled = [
                pltpu.roll(own_ref[lev, 8 * q : 8 * q + 8, LANES * b : LANES * b + LANES], HALO, axis=1)
                for b in range(8)
            ]
            shifted = [jnp.where(lane < HALO, rolled[b - 1], rolled[b]) for b in range(8)]
            turned.append(
                [
                    [pltpu.roll(block, 32 * n, axis=1) if n else block for n in range(4)]
                    for block in shifted
                ]
            )

        for b in range(8):
            for k in range(4):
                at = 12 * (32 * lev + 4 * b + k)
                near = [turned[q][b][(q - k) % 4] for q in range(4)]
                after = near if k < 3 else [turned[q][(b + 1) % 8][(q - k) % 4] for q in range(4)]
                pieces_ref[at + 4 : at + 12] = in_groups(near)
                rest = in_groups(after[3:] + after[:3])
                other = pltpu.roll(rest, 16, axis=1)
                pieces_ref[at : at + 4] = jnp.where(lane[0:4] % 32 < 16, rest[0:4], other[4:8])


def in_groups(parts):
    group = lane_of(parts[0].shape) // 32
    out = parts[0]
    for q in range(1, 4):
        out = jnp.where(group == q, parts[q], out)
    return out


def fields_body(chunk_ref, bg_ref, lon_ref, lat_ref, fields_ref):
    chunk = chunk_ref[0]
    lev, b, k = chunk // 32, chunk % 32 // 4, chunk % 4
    wide = lane_of((CY, LANES))

    def block(ref, index):
        return ref[lev, :, pl.ds(pl.multiple_of(index * LANES, LANES), LANES)]

    for index, ref in enumerate((bg_ref, lon_ref, lat_ref)):
        mid = block(ref, b)
        mid = jnp.where((wide >= LANES - HALO) & (k == 0), block(ref, (b + 7) % 8), mid)
        mid = jnp.where((wide < HALO) & (k == 3), block(ref, (b + 1) % 8), mid)
        mid = pltpu.roll(mid, (HALO - CHUNK * k + LANES) % LANES, axis=1)
        mid = jnp.where(wide < CHUNK + 2 * HALO, mid, 0.0)
        fields_ref[index] = jnp.where(wide < 64, mid, pltpu.roll(mid, 64, axis=1))


def edges_body(even_ref, x_ref, fields_ref, near_ref, far_ref):
    even = even_ref[0] == 1

    def put(at, count, low, high):
        near_ref[at : at + count] = jnp.where(even, high, low)
        far_ref[at : at + count] = jnp.where(even, low, high)

    for u in range(MEMBERS // 4):
        for row, count in ((0, 4), (4, 8)):
            lows, highs = [], []
            for i in range(4):
                at = 12 * (4 * u + i) + row
                piece = x_ref[at : at + count]
                lows.append(pltpu.roll(piece, 32 * i, axis=1) if i else piece)
                highs.append(pltpu.roll(piece, 32 * i + 32, axis=1) if i < 3 else piece)
            if row == 0:
                lows, highs = lows[3:] + lows[:3], highs[3:] + highs[:3]
            put(12 * u + row, count, in_groups(lows), in_groups(highs))
    for index in range(3):
        at = EDGE - 3 * HALO + HALO * index
        put(at, HALO, fields_ref[index, 0:HALO], fields_ref[index, CY - HALO : CY])


def unpacked(ref, first, second):
    lane = lane_of((8, LANES))
    place = lane % 64
    mains, rests = [], []
    for at, turn in ((first, 0), (second, 64)):
        rest = ref[pl.ds(at, 4)]
        rest = jnp.concatenate([rest, pltpu.roll(rest, LANES - 16, axis=1)], axis=0)
        main = ref[pl.ds(at + 4, 8)]
        mains.append(pltpu.roll(main, turn, axis=1) if turn else main)
        rests.append(pltpu.roll(rest, turn, axis=1) if turn else rest)
    sources = [mains[0], rests[0], mains[1], rests[1]]
    out = []
    for q in range(4):
        whole = in_groups([sources[(group - q) % 4] for group in range(4)])
        whole = pltpu.roll(whole, LANES - 32 * q, axis=1) if q else whole
        out.append(jnp.where(place < CHUNK + 2 * HALO, whole, 0.0))
    return out


def advance(state, south, north, coefs, at):
    west_c, east_c, south_c, north_c, own_c = (ref[at : at + 8] for ref in coefs)
    west = pltpu.roll(state, 1, axis=1)
    east = pltpu.roll(state, LANES - 1, axis=1)
    speed = 0.85 + 0.15 * jnp.tanh(state)
    change = west_c * west + east_c * east
    change = change + (south_c * south + north_c * north)
    return state + speed * (change - own_c * state)


def inside_body(x_ref, fields_ref, mid_ref, steps_ref, seen_ref, total_ref, *coefs):
    fill_coefs(fields_ref[1], fields_ref[2], coefs)
    total_ref[...] = jnp.zeros((CY - 2 * HALO, LANES), jnp.float32)

    edge = jnp.zeros((HALO, LANES), jnp.float32)

    def one(index, carry):
        pairs = [index * GROUP + p for p in range(GROUP)]
        for p in pairs:
            for step in range(NSTEP):
                steps_ref[step, p, 0:HALO] = edge
                steps_ref[step, p, HALO + CY : ROWS] = edge
            for q, out in enumerate(unpacked(x_ref, 12 * p, 12 * (p + PAIRS))):
                rows = slice(8 * q, 8 * q + 8)
                mid_ref[p, rows] = out
                steps_ref[0, p, HALO + 8 * q : HALO + 8 * q + 8] = fields_ref[0, rows] + 0.5 * out
        for step in range(NSTEP):
            for q in range(4) if step < NSTEP - 1 else (1, 2):
                at = 8 * q
                for p in pairs:
                    now = steps_ref.at[step, p]
                    put = HALO + at
                    state = advance(
                        now[put : put + 8], now[put - 1 : put + 7], now[put + 1 : put + 9], coefs, at
                    )
                    if step < NSTEP - 1:
                        steps_ref[step + 1, p, put : put + 8] = state
                    else:
                        seen = state + 0.25 * state * state
                        seen_ref[p, at - 8 : at] = seen
                        total_ref[at - 8 : at] += seen
        return carry

    lax.fori_loop(0, PAIRS // GROUP, one, 0)


def cells_body(chunk_ref, value_ref, weight_ref, column_ref, level_ref, out_ref):
    chunk = chunk_ref[0]
    column = column_ref[...]
    row = column // NX
    offset = column % NX - CHUNK * (chunk % 32)
    inside = (offset >= 0) & (offset < CHUNK) & (level_ref[...] == chunk // 32)
    lane = jnp.where(inside, HALO + offset, -1)
    square = weight_ref[...] * weight_ref[...]
    nobs = column.shape[1]
    at_row = lax.broadcasted_iota(jnp.int32, (CY, nobs), 0) == row
    at_lane = (lax.broadcasted_iota(jnp.int32, (LANES, nobs), 0) == lane).astype(jnp.bfloat16)
    parts = []
    for value in (square, square * value_ref[...]):
        left = jnp.where(at_row, value, 0.0)
        for _ in range(3):
            part = left.astype(jnp.bfloat16)
            parts.append(part)
            left = left - part.astype(jnp.float32)
    sums = lax.dot_general(
        jnp.concatenate(parts, axis=0),
        at_lane,
        (((1,), (1,)), ((), ())),
        preferred_element_type=jnp.float32,
    )
    for index in range(2):
        base = 3 * CY * index
        total = sums[base : base + CY] + sums[base + CY : base + 2 * CY]
        total = total + sums[base + 2 * CY : base + 3 * CY]
        out_ref[index] = total


def transport(base, anoms, coefs, buf_ref, first, use):
    for p in range(GROUP):
        at = HALO
        for ref in anoms:
            rows = ref.shape[1]
            buf_ref[0, p, at : at + rows] = base[at - HALO : at - HALO + rows] + 0.5 * ref[first + p]
            at += rows
    for step in range(NSTEP):
        for low in range(0, ROWS, 8) if step < NSTEP - 1 else range(HALO, HALO + CY, 8):
            at = HALO + low
            for p in range(GROUP):
                now = buf_ref.at[step % 2, p]
                state = advance(
                    now[at : at + 8], now[at - 1 : at + 7], now[at + 1 : at + 9], coefs, low
                )
                if step < NSTEP - 1:
                    buf_ref[(step + 1) % 2, p, at : at + 8] = state
                else:
                    use(first + p, low - HALO, state)


def edge_transport(base, low_ref, high_ref, coefs, steps_ref, buf_ref, use):
    for p in range(PAIRS):
        buf_ref[0, p, 0:HALO] = base[0:HALO] + 0.5 * low_ref[p]
        buf_ref[1, p, 2 * HALO : 3 * HALO] = base[HALO + CY :] + 0.5 * high_ref[p]
    for step in range(NSTEP):
        for edge in range(2):
            inside, put, at, low = (
                (HALO + step, step + 8, step + 1, step + 1)
                if edge == 0
                else (CY - step, 8 - step, 15 - step, 39 - step)
            )
            for p in range(PAIRS):
                now = buf_ref.at[edge, p]
                now[put : put + 8] = steps_ref[step, p, inside : inside + 8]
                state = advance(
                    now[at : at + 8], now[at - 1 : at + 7], now[at + 1 : at + 9], coefs, low
                )
                if step < NSTEP - 1:
                    now[at : at + 8] = state
                else:
                    use(p, (CY - HALO) * edge, state)


def blocks(rows):
    return [rows[8 * q : 8 * q + 8] for q in range(4)]


def inner(rows, start):
    lane = lane_of((8, LANES))
    out = None
    for q in range(4):
        moved = pltpu.roll(rows[q], (32 * q - HALO - start) % LANES, axis=1)
        out = moved if out is None else jnp.where(lane >= 32 * q, moved, out)
    return out


def observer(total_ref, obs_ref):
    def use(p, row, state):
        seen = state + 0.25 * state * state
        obs_ref[p, row : row + 8] = seen
        total_ref[row : row + 8] += seen

    return use


def for_groups(work):
    def one(index, carry):
        work(index * GROUP)
        return carry

    lax.fori_loop(0, PAIRS // GROUP, one, 0)


def normal_terms(rows_of, total, cells_ref, gram_ref, dev_ref, left_ref, right_ref):
    center = (total + pltpu.roll(total, 64, axis=1)) * (1.0 / MEMBERS)
    for p in range(PAIRS):
        dev = [rows - center[8 * q : 8 * q + 8] for q, rows in enumerate(rows_of(p))]
        for half in range(2):
            at = 8 * (p + PAIRS * half)
            dev_ref[at : at + 8] = inner(dev, 64 * half)
    weight, weighted = cells_ref[0], cells_ref[1]
    aim = inner(blocks(2.0 * (weighted - weight * center)), 0)
    weight = inner(blocks(4.0 * weight), 0)
    right_ref[MEMBERS:LANES, :] = jnp.zeros((LANES - MEMBERS, 8 * LANES), jnp.float32)
    for r in range(8):
        rows = dev_ref[pl.ds(r, MEMBERS, stride=8), :]
        left_ref[:, LANES * r : LANES * r + LANES] = rows
        right_ref[0:MEMBERS, LANES * r : LANES * r + LANES] = rows * weight[r : r + 1]
        right_ref[MEMBERS : MEMBERS + 1, LANES * r : LANES * r + LANES] = aim[r : r + 1]
    gram = lax.dot_general(
        left_ref[...],
        right_ref[...],
        (((1,), (1,)), ((), ())),
        precision=HIGHEST,
        preferred_element_type=jnp.float32,
    )
    wide = lane_of((MEMBERS, LANES))
    sub = lax.broadcasted_iota(jnp.int32, (MEMBERS, LANES), 0)
    column = jnp.broadcast_to(gram[:, MEMBERS : MEMBERS + 1], (MEMBERS, LANES))
    project = jnp.sum(jnp.where(wide == sub, column, 0.0), axis=0, keepdims=True)
    top, bottom = gram[0:PAIRS], gram[PAIRS:MEMBERS]
    lane, sub = wide[0:PAIRS], sub[0:PAIRS]
    diagonal = jnp.sum(jnp.where(lane - 32 == sub, bottom, 0.0), axis=0, keepdims=True)
    square = jnp.where(lane - 32 >= sub, pltpu.roll(top, 32, axis=1), bottom)
    square = jnp.where(lane < 32, pltpu.roll(top, LANES - 32, axis=1), square)
    packed = jnp.where(lane[0:16] < 64, square[0:16], pltpu.roll(square[16:32], 64, axis=1))
    gram_ref[...] = jnp.zeros((PACKED, LANES), jnp.float32)
    gram_ref[0:8] = packed[0:8]
    gram_ref[8:9] = jnp.where(lane[0:1] < 64, project, pltpu.roll(diagonal, 32, axis=1))
    gram_ref[10:18] = packed[8:16]


def fill_coefs(lon, lat, coefs):
    west_c, east_c, south_c, north_c, own_c = coefs
    west_c[...] = jnp.maximum(lon, 0.0)
    east_c[...] = jnp.maximum(-lon, 0.0)
    south_c[...] = jnp.maximum(lat, 0.0)
    north_c[...] = jnp.maximum(-lat, 0.0)
    own_c[...] = jnp.abs(lon) + jnp.abs(lat)


def first_body(
    even_ref, far_ref, near_ref, fields_ref, steps_ref, seen_ref, total_ref, cells_ref,
    gram_ref, south_ref, north_ref, full_ref, low_ref, high_ref, buf_ref, sum_ref, obs_ref, *scratch
):
    even = even_ref[0] == 1
    near, far = near_ref[...], far_ref[...]
    low_ref[...] = jnp.where(even, far, near)
    high_ref[...] = jnp.where(even, near, far)
    coefs, rest = scratch[:5], scratch[5:]
    for index in range(3):
        at = EDGE - 3 * HALO + HALO * index
        full_ref[index, 0:HALO] = low_ref[at : at + HALO]
        full_ref[index, HALO : HALO + CY] = fields_ref[index]
        full_ref[index, HALO + CY : ROWS] = high_ref[at : at + HALO]
    fill_coefs(full_ref[1], full_ref[2], coefs)
    sum_ref[0:HALO] = jnp.zeros((HALO, LANES), jnp.float32)
    sum_ref[HALO : CY - HALO] = total_ref[...]
    sum_ref[CY - HALO : CY] = jnp.zeros((HALO, LANES), jnp.float32)
    use = observer(sum_ref, obs_ref)
    base = full_ref[0]

    for ref, out_ref in ((low_ref, south_ref), (high_ref, north_ref)):
        for u in range(PAIRS // 4):
            for i, rows in enumerate(unpacked(ref, 12 * u, 12 * (u + PAIRS // 4))):
                out_ref[4 * u + i] = rows
    edge_transport(base, south_ref, north_ref, coefs, steps_ref, buf_ref, use)

    def rows_of(p):
        return [obs_ref[p, 0:8], seen_ref[p, 0:8], seen_ref[p, 8:16], obs_ref[p, 24:32]]

    normal_terms(rows_of, sum_ref[...], cells_ref, gram_ref, *rest)


def solve(packed, weights):
    shape = (MEMBERS, LANES)
    wide = lane_of(shape)
    sub = lax.broadcasted_iota(jnp.int32, shape, 0)
    left = MEMBERS - 1.0
    low, high = packed[0], packed[1]
    packed = jnp.concatenate([low[0:8], high[0:8]], axis=0)
    ends = jnp.broadcast_to(low[8:9], shape)
    square = jnp.concatenate([packed, pltpu.roll(packed, 64, axis=1)], axis=0)
    padded = jnp.concatenate([square, jnp.zeros((LANES - PAIRS, LANES), jnp.float32)], axis=0)
    turned = jnp.transpose(padded)
    lane, row = wide[0:PAIRS], sub[0:PAIRS]
    top = jnp.where(lane >= row, pltpu.roll(square, LANES - 32, axis=1), turned[32:64])
    top = jnp.where(lane < 32, top, pltpu.roll(square, 32, axis=1))
    bottom = jnp.where(lane - 32 < row, square, pltpu.roll(turned[32:64], 32, axis=1))
    bottom = jnp.where(lane - 32 == row, pltpu.roll(ends, LANES - 32, axis=1)[0:PAIRS], bottom)
    bottom = jnp.where(lane < 32, turned[0:32], bottom)
    sums = jnp.concatenate([top, bottom], axis=0)
    project = jnp.sum(jnp.where(wide == sub, ends, 0.0), axis=1, keepdims=True)
    gradient = left * weights - jnp.broadcast_to(project, shape)
    lane = wide
    matrix = jnp.where(
        lane < MEMBERS,
        sums + jnp.where(lane == sub, left, 0.0),
        jnp.where(lane == MEMBERS, gradient, 0.0),
    )
    width = 8
    for start in range(0, MEMBERS, width):
        columns = [
            jnp.broadcast_to(matrix[:, start + j : start + j + 1], shape) for j in range(width)
        ]
        for j in range(width):
            k = start + j
            factor = jnp.where(sub == k, 0.0, columns[j] * (1.0 / columns[j][k : k + 1]))
            for later in range(j + 1, width):
                columns[later] = columns[later] - factor * columns[later][k : k + 1]
            matrix = matrix - factor * matrix[k : k + 1]
    diagonal = jnp.sum(jnp.where(lane == sub, matrix, 0.0), axis=1, keepdims=True)
    solved = matrix[:, MEMBERS : MEMBERS + 1] / diagonal
    return weights - jnp.broadcast_to(solved, shape)


def by_pair(weights):
    lane = lane_of((PAIRS, LANES))
    return jnp.where(lane < 64, weights[0:PAIRS], weights[PAIRS:MEMBERS])


def mix(pair_ref, anoms_ref):
    total = jnp.zeros(anoms_ref.shape[1:], jnp.float32)
    for p in range(PAIRS):
        total = total + pair_ref[p : p + 1] * anoms_ref[p]
    return total + pltpu.roll(total, 64, axis=1)


def second_body(
    sums_ref, south_ref, mid_ref, north_ref, full_ref, cells_ref,
    gram_ref, weights_ref, pair_ref, buf_ref, sum_ref, obs_ref, *scratch
):
    coefs, rest = scratch[:5], scratch[5:]
    fill_coefs(full_ref[1], full_ref[2], coefs)
    weights = solve(sums_ref[...], jnp.zeros((MEMBERS, LANES), jnp.float32))
    weights_ref[...] = weights
    pair_ref[...] = by_pair(weights)
    anoms = (south_ref, mid_ref, north_ref)
    base = full_ref[0] + jnp.concatenate([mix(pair_ref, ref) for ref in anoms], axis=0)
    edge = jnp.zeros((2, GROUP, HALO, LANES), jnp.float32)
    buf_ref[:, :, 0:HALO] = edge
    buf_ref[:, :, HALO + ROWS :] = edge
    sum_ref[...] = jnp.zeros((CY, LANES), jnp.float32)
    use = observer(sum_ref, obs_ref)
    for_groups(lambda first: transport(base, anoms, coefs, buf_ref, first, use))
    normal_terms(
        lambda p: blocks(obs_ref[p]), sum_ref[...], cells_ref, gram_ref, *rest
    )


def last_body(sums_ref, weights_ref, mid_ref, out_ref, pair_ref):
    weights = solve(sums_ref[...], weights_ref[...])
    pair_ref[...] = by_pair(weights)
    out_ref[...] = inner(blocks(mix(pair_ref, mid_ref)), 0)


def spread_body(pieces_ref, out_ref):
    lane = lane_of((8, LANES))
    for lev in range(LEV):
        for b in range(8):
            pieces = [pieces_ref[k % 2, 16 * lev + 2 * b + k // 2] for k in range(4)]
            for q in range(4):
                out = None
                for k in range(4):
                    moved = pltpu.roll(pieces[k], (32 * (k - q)) % LANES, axis=1)
                    out = moved if out is None else jnp.where(lane >= 32 * k, moved, out)
                out_ref[lev, 8 * q : 8 * q + 8, LANES * b : LANES * b + LANES] = out


def exchange(array, axes):
    return lax.all_to_all(array, axes, 0, 0, tiled=True)


def to_all(array, axes, count):
    return exchange(jnp.broadcast_to(array[None], (count, *array.shape)), axes)


def both_cores(array):
    return lax.all_gather(array, "core")


def sum_everywhere(packed):
    shape = (5, 2, LANES)
    halves = jnp.broadcast_to(packed.reshape(1, 2, 1, *shape), (2, 2, 8, *shape))
    part = jnp.sum(exchange(halves.reshape(32, *shape), PLANE), axis=0)
    part = jnp.sum(to_all(part, "z", 16), axis=0).reshape(10, LANES)
    return both_cores(part)


def local(
    background, anomalies, courant_lon, courant_lat, obs_value, obs_weight, obs_column, obs_level
):
    chunk = lax.axis_index(MEM).astype(jnp.int32).reshape(1)
    pieces = call(pack_body, f32(MEMBERS * 12, LANES), in_specs=[VMEM])(anomalies[0])
    pieces = exchange(pieces.reshape(MEMBERS, 3, 4, LANES), MEM).reshape(MEMBERS * 12, LANES)
    nobs = obs_value.shape[0]
    flat = [a.reshape(1, nobs) for a in (obs_value, obs_weight, obs_column, obs_level)]
    cells = call(cells_body, f32(2, CY, LANES), in_specs=[SMEM] + [VMEM] * 4)(chunk, *flat)
    fields = call(fields_body, f32(3, CY, LANES), in_specs=[SMEM] + [VMEM] * 3)(
        chunk, background, courant_lon, courant_lat
    )
    pieces, fields, cells = lax.optimization_barrier((pieces, fields, cells))
    even = (1 - lax.axis_index("x") % 2).astype(jnp.int32).reshape(1)
    near_edge, far_edge = call(
        edges_body, (f32(EDGE, LANES), f32(EDGE, LANES)), in_specs=[SMEM] + [VMEM] * 2
    )(even, pieces, fields)
    far = lax.ppermute(far_edge, TILE, [(t, t + 1 if t % 2 else t - 1) for t in range(1, 7)])
    near = lax.ppermute(near_edge, TILE, [(t, t - 1 if t % 2 else t + 1) for t in range(8)])
    mid, steps, seen, total = call(
        inside_body,
        (
            f32(PAIRS, CY, LANES),
            f32(NSTEP, PAIRS, ROWS, LANES),
            f32(PAIRS, CY - 2 * HALO, LANES),
            f32(CY - 2 * HALO, LANES),
        ),
        [pltpu.VMEM((CY, LANES), jnp.float32)] * 5,
        in_specs=[VMEM] * 2,
    )(pieces, fields)
    rest = [
        pltpu.VMEM((CY, LANES), jnp.float32),
        pltpu.VMEM((PAIRS, CY, LANES), jnp.float32),
        *[pltpu.VMEM((ROWS, LANES), jnp.float32)] * 5,
        pltpu.VMEM((MEMBERS * 8, LANES), jnp.float32),
        pltpu.VMEM((MEMBERS, 8 * LANES), jnp.float32),
        pltpu.VMEM((LANES, 8 * LANES), jnp.float32),
    ]
    pair = pltpu.VMEM((PAIRS, LANES), jnp.float32)
    gram, south, north, full = call(
        first_body,
        (f32(PACKED, LANES), *[f32(PAIRS, HALO, LANES)] * 2, f32(3, ROWS, LANES)),
        [
            *[pltpu.VMEM((EDGE, LANES), jnp.float32)] * 2,
            pltpu.VMEM((2, PAIRS, 3 * HALO, LANES), jnp.float32),
            *rest,
        ],
        in_specs=[SMEM] + [VMEM] * 7,
    )(even, far, near, fields, steps, seen, total, cells)
    gram, weights = call(
        second_body,
        (f32(PACKED, LANES), f32(MEMBERS, LANES)),
        [pair, pltpu.VMEM((2, GROUP, ROWS + 2 * HALO, LANES), jnp.float32), *rest],
        in_specs=[VMEM] * 6,
    )(sum_everywhere(gram), south, mid, north, full, cells)
    part = call(last_body, f32(8, LANES), [pair], in_specs=[VMEM] * 3)(
        sum_everywhere(gram), weights, mid
    )
    parts = both_cores(to_all(part, ("z", "yl"), 32))
    return call(spread_body, f32(LEV, CY, NX), in_specs=[VMEM])(parts)


def solution(mesh):
    fine = Mesh(mesh.devices.reshape(16, 2, 2, 2, 4), ("z", "yl", "core", "yh", "x"))
    return jax.shard_map(
        local,
        mesh=fine,
        in_specs=(
            P(None, TILE, None),
            P(MEM, None, TILE, None),
            P(None, TILE, None),
            P(None, TILE, None),
            P(TILE),
            P(TILE),
            P(TILE),
            P(TILE),
        ),
        out_specs=P(None, TILE, None),
        check_vma=False,
    )
```

```python
import functools

import jax
import jax.numpy as jnp
from jax import lax
from jax.experimental import pallas as pl
from jax.experimental.pallas import tpu as pltpu
from jax.sharding import Mesh, PartitionSpec as P

NSTEP = 8
MEMBERS = 64
PAIRS = 32
GROUP = 16
LEV = 2
CY = 32
NX = 1024
CHUNK = 32
HALO = 8
ROWS = CY + 2 * HALO
EDGE = 12 * MEMBERS // 4
LANES = 128
PACKED = 20

MEM = ("z", "yl", "core")
TILE = ("yh", "x")
PLANE = ("yl", "core", "yh", "x")
VMEM = pl.BlockSpec(memory_space=pltpu.VMEM)
SMEM = pl.BlockSpec(memory_space=pltpu.SMEM)


def lane_of(shape):
    return lax.broadcasted_iota(jnp.int32, shape, len(shape) - 1)


def call(body, out, scratch=(), in_specs=None, vmem=40 << 20):
    return pl.pallas_call(
        body,
        out_shape=out,
        in_specs=in_specs,
        out_specs=jax.tree.map(lambda _: VMEM, out),
        scratch_shapes=list(scratch),
        compiler_params=pltpu.CompilerParams(vmem_limit_bytes=vmem),
    )


def f32(*shape):
    return jax.ShapeDtypeStruct(shape, jnp.float32)


def pack_body(own_ref, pieces_ref):
    lane = lane_of((8, LANES))
    for lev in range(LEV):
        turned = []
        for q in range(4):
            rolled = [
                pltpu.roll(own_ref[lev, 8 * q : 8 * q + 8, LANES * b : LANES * b + LANES], HALO, axis=1)
                for b in range(8)
            ]
            shifted = [jnp.where(lane < HALO, rolled[b - 1], rolled[b]) for b in range(8)]
            turned.append(
                [
                    [pltpu.roll(block, 32 * n, axis=1) if n else block for n in range(4)]
                    for block in shifted
                ]
            )

        for b in range(8):
            for k in range(4):
                at = 12 * (32 * lev + 4 * b + k)
                near = [turned[q][b][(q - k) % 4] for q in range(4)]
                after = near if k < 3 else [turned[q][(b + 1) % 8][(q - k) % 4] for q in range(4)]
                pieces_ref[at + 4 : at + 12] = in_groups(near)
                rest = in_groups(after[3:] + after[:3])
                other = pltpu.roll(rest, 16, axis=1)
                pieces_ref[at : at + 4] = jnp.where(lane[0:4] % 32 < 16, rest[0:4], other[4:8])


def in_groups(parts):
    group = lane_of(parts[0].shape) // 32
    out = parts[0]
    for q in range(1, 4):
        out = jnp.where(group == q, parts[q], out)
    return out


def fields_body(chunk_ref, even_ref, bg_ref, lon_ref, lat_ref, fields_ref, near_ref, far_ref):
    chunk, even = chunk_ref[0], even_ref[0] == 1
    lev, b, k = chunk // 32, chunk % 32 // 4, chunk % 4
    wide = lane_of((CY, LANES))

    def block(ref, index):
        return ref[lev, :, pl.ds(pl.multiple_of(index * LANES, LANES), LANES)]

    for index, ref in enumerate((bg_ref, lon_ref, lat_ref)):
        mid = block(ref, b)
        mid = jnp.where((wide >= LANES - HALO) & (k == 0), block(ref, (b + 7) % 8), mid)
        mid = jnp.where((wide < HALO) & (k == 3), block(ref, (b + 1) % 8), mid)
        mid = pltpu.roll(mid, (HALO - CHUNK * k + LANES) % LANES, axis=1)
        mid = jnp.where(wide < CHUNK + 2 * HALO, mid, 0.0)
        mid = jnp.where(wide < 64, mid, pltpu.roll(mid, 64, axis=1))
        fields_ref[index] = mid
        near_ref[index] = jnp.where(even, mid[CY - HALO :], mid[:HALO])
        far_ref[index] = jnp.where(even, mid[:HALO], mid[CY - HALO :])


def edges_body(even_ref, x_ref, near_ref, far_ref):
    even = even_ref[0] == 1

    def put(at, count, low, high):
        near_ref[at : at + count] = jnp.where(even, high, low)
        far_ref[at : at + count] = jnp.where(even, low, high)

    for u in range(MEMBERS // 4):
        for row, count in ((0, 4), (4, 8)):
            lows, highs = [], []
            for i in range(4):
                at = 12 * (4 * u + i) + row
                piece = x_ref[at : at + count]
                lows.append(pltpu.roll(piece, 32 * i, axis=1) if i else piece)
                highs.append(pltpu.roll(piece, 32 * i + 32, axis=1) if i < 3 else piece)
            if row == 0:
                lows, highs = lows[3:] + lows[:3], highs[3:] + highs[:3]
            put(12 * u + row, count, in_groups(lows), in_groups(highs))


def unpacked(ref, first, second):
    lane = lane_of((8, LANES))
    place = lane % 64
    mains, rests = [], []
    for at, turn in ((first, 0), (second, 64)):
        rest = ref[pl.ds(at, 4)]
        rest = jnp.concatenate([rest, pltpu.roll(rest, LANES - 16, axis=1)], axis=0)
        main = ref[pl.ds(at + 4, 8)]
        mains.append(pltpu.roll(main, turn, axis=1) if turn else main)
        rests.append(pltpu.roll(rest, turn, axis=1) if turn else rest)
    sources = [mains[0], rests[0], mains[1], rests[1]]
    out = []
    for q in range(4):
        whole = in_groups([sources[(group - q) % 4] for group in range(4)])
        whole = pltpu.roll(whole, LANES - 32 * q, axis=1) if q else whole
        out.append(jnp.where(place < CHUNK + 2 * HALO, whole, 0.0))
    return out


def advance(state, south, north, coefs, at):
    west_c, east_c, south_c, north_c, own_c = (ref[at : at + 8] for ref in coefs)
    west = pltpu.roll(state, 1, axis=1)
    east = pltpu.roll(state, LANES - 1, axis=1)
    speed = 0.85 + 0.15 * jnp.tanh(state)
    change = west_c * west + east_c * east
    change = change + (south_c * south + north_c * north)
    return state + speed * (change - own_c * state)


def inside_body(x_ref, fields_ref, mid_ref, steps_ref, seen_ref, total_ref, *coefs):
    fill_coefs(fields_ref[1], fields_ref[2], coefs)
    total_ref[...] = jnp.zeros((CY - 2 * HALO, LANES), jnp.float32)

    edge = jnp.zeros((HALO, LANES), jnp.float32)

    def one(index, carry):
        pairs = [index * GROUP + p for p in range(GROUP)]
        for p in pairs:
            for step in range(NSTEP):
                steps_ref[step, p, 0:HALO] = edge
                steps_ref[step, p, HALO + CY : ROWS] = edge
            for q, out in enumerate(unpacked(x_ref, 12 * p, 12 * (p + PAIRS))):
                rows = slice(8 * q, 8 * q + 8)
                mid_ref[p, rows] = out
                steps_ref[0, p, HALO + 8 * q : HALO + 8 * q + 8] = fields_ref[0, rows] + 0.5 * out
        for step in range(NSTEP):
            for q in range(4) if step < NSTEP - 1 else (1, 2):
                at = 8 * q
                for p in pairs:
                    now = steps_ref.at[step, p]
                    put = HALO + at
                    state = advance(
                        now[put : put + 8], now[put - 1 : put + 7], now[put + 1 : put + 9], coefs, at
                    )
                    if step < NSTEP - 1:
                        steps_ref[step + 1, p, put : put + 8] = state
                    else:
                        seen = state + 0.25 * state * state
                        seen_ref[p, at - 8 : at] = seen
                        total_ref[at - 8 : at] += seen
        return carry

    lax.fori_loop(0, PAIRS // GROUP, one, 0)


def cells_body(chunk_ref, value_ref, weight_ref, column_ref, level_ref, out_ref):
    chunk = chunk_ref[0]
    column = column_ref[...]
    row = column // NX
    offset = column % NX - CHUNK * (chunk % 32)
    inside = (offset >= 0) & (offset < CHUNK) & (level_ref[...] == chunk // 32)
    lane = jnp.where(inside, HALO + offset, -1)
    square = weight_ref[...] * weight_ref[...]
    nobs = column.shape[1]
    at_row = lax.broadcasted_iota(jnp.int32, (CY, nobs), 0) == row
    at_lane = (lax.broadcasted_iota(jnp.int32, (LANES, nobs), 0) == lane).astype(jnp.bfloat16)
    parts = []
    for value in (square, square * value_ref[...]):
        left = jnp.where(at_row, value, 0.0)
        for _ in range(3):
            part = left.astype(jnp.bfloat16)
            parts.append(part)
            left = left - part.astype(jnp.float32)
    sums = lax.dot_general(
        jnp.concatenate(parts, axis=0),
        at_lane,
        (((1,), (1,)), ((), ())),
        preferred_element_type=jnp.float32,
    )
    for index in range(2):
        base = 3 * CY * index
        total = sums[base : base + CY] + sums[base + CY : base + 2 * CY]
        total = total + sums[base + 2 * CY : base + 3 * CY]
        out_ref[index] = total


def transport(base, anoms, coefs, buf_ref, first, use):
    for p in range(GROUP):
        at = HALO
        for ref in anoms:
            rows = ref.shape[1]
            buf_ref[0, p, at : at + rows] = base[at - HALO : at - HALO + rows] + 0.5 * ref[first + p]
            at += rows
    for step in range(NSTEP):
        for low in range(0, ROWS, 8) if step < NSTEP - 1 else range(HALO, HALO + CY, 8):
            at = HALO + low
            for p in range(GROUP):
                now = buf_ref.at[step % 2, p]
                state = advance(
                    now[at : at + 8], now[at - 1 : at + 7], now[at + 1 : at + 9], coefs, low
                )
                if step < NSTEP - 1:
                    buf_ref[(step + 1) % 2, p, at : at + 8] = state
                else:
                    use(first + p, low - HALO, state)


def edge_transport(base, low_ref, high_ref, coefs, steps_ref, buf_ref, use):
    for p in range(PAIRS):
        buf_ref[0, p, 0:HALO] = base[0:HALO] + 0.5 * low_ref[p]
        buf_ref[1, p, 2 * HALO : 3 * HALO] = base[HALO + CY :] + 0.5 * high_ref[p]
    for step in range(NSTEP):
        for edge in range(2):
            inside, put, at, low = (
                (HALO + step, step + 8, step + 1, step + 1)
                if edge == 0
                else (CY - step, 8 - step, 15 - step, 39 - step)
            )
            for p in range(PAIRS):
                now = buf_ref.at[edge, p]
                now[put : put + 8] = steps_ref[step, p, inside : inside + 8]
                state = advance(
                    now[at : at + 8], now[at - 1 : at + 7], now[at + 1 : at + 9], coefs, low
                )
                if step < NSTEP - 1:
                    now[at : at + 8] = state
                else:
                    use(p, (CY - HALO) * edge, state)


def blocks(rows):
    return [rows[8 * q : 8 * q + 8] for q in range(4)]


def inner(rows, start):
    lane = lane_of((8, LANES))
    out = None
    for q in range(4):
        moved = pltpu.roll(rows[q], (32 * q - HALO - start) % LANES, axis=1)
        out = moved if out is None else jnp.where(lane >= 32 * q, moved, out)
    return out


def observer(total_ref, obs_ref):
    def use(p, row, state):
        seen = state + 0.25 * state * state
        obs_ref[p, row : row + 8] = seen
        total_ref[row : row + 8] += seen

    return use


def for_groups(work):
    def one(index, carry):
        work(index * GROUP)
        return carry

    lax.fori_loop(0, PAIRS // GROUP, one, 0)


def split(value):
    high = value.astype(jnp.bfloat16)
    return high, (value - high.astype(jnp.float32)).astype(jnp.bfloat16)


def by_rows(left, right):
    return lax.dot_general(
        left, right, (((1,), (1,)), ((), ())), preferred_element_type=jnp.float32
    )


def normal_terms(rows_of, total, cells_ref, gram_ref, dev_ref, left_ref, right_ref):
    center = (total + pltpu.roll(total, 64, axis=1)) * (1.0 / MEMBERS)
    for p in range(PAIRS):
        dev = [rows - center[8 * q : 8 * q + 8] for q, rows in enumerate(rows_of(p))]
        for half in range(2):
            at = 8 * (p + PAIRS * half)
            dev_ref[at : at + 8] = inner(dev, 64 * half)
    weight, weighted = cells_ref[0], cells_ref[1]
    aim = inner(blocks(2.0 * (weighted - weight * center)), 0)
    weight = inner(blocks(4.0 * weight), 0)
    right_ref[MEMBERS:LANES, :] = jnp.zeros((LANES - MEMBERS, 8 * LANES), jnp.float32)
    for r in range(8):
        rows = dev_ref[pl.ds(r, MEMBERS, stride=8), :]
        left_ref[:, LANES * r : LANES * r + LANES] = rows
        right_ref[0:MEMBERS, LANES * r : LANES * r + LANES] = rows * weight[r : r + 1]
        right_ref[MEMBERS : MEMBERS + 1, LANES * r : LANES * r + LANES] = aim[r : r + 1]
    (left_high, left_low), (right_high, right_low) = split(left_ref[...]), split(right_ref[...])
    gram = by_rows(left_high, right_high)
    gram = gram + (by_rows(left_high, right_low) + by_rows(left_low, right_high))
    wide = lane_of((MEMBERS, LANES))
    sub = lax.broadcasted_iota(jnp.int32, (MEMBERS, LANES), 0)
    column = jnp.broadcast_to(gram[:, MEMBERS : MEMBERS + 1], (MEMBERS, LANES))
    project = jnp.sum(jnp.where(wide == sub, column, 0.0), axis=0, keepdims=True)
    top, bottom = gram[0:PAIRS], gram[PAIRS:MEMBERS]
    lane, sub = wide[0:PAIRS], sub[0:PAIRS]
    diagonal = jnp.sum(jnp.where(lane - 32 == sub, bottom, 0.0), axis=0, keepdims=True)
    square = jnp.where(lane - 32 >= sub, pltpu.roll(top, 32, axis=1), bottom)
    square = jnp.where(lane < 32, pltpu.roll(top, LANES - 32, axis=1), square)
    packed = jnp.where(lane[0:16] < 64, square[0:16], pltpu.roll(square[16:32], 64, axis=1))
    gram_ref[...] = jnp.zeros((PACKED, LANES), jnp.float32)
    gram_ref[0:8] = packed[0:8]
    gram_ref[8:9] = jnp.where(lane[0:1] < 64, project, pltpu.roll(diagonal, 32, axis=1))
    gram_ref[10:18] = packed[8:16]


def fill_coefs(lon, lat, coefs):
    west_c, east_c, south_c, north_c, own_c = coefs
    west_c[...] = jnp.maximum(lon, 0.0)
    east_c[...] = jnp.maximum(-lon, 0.0)
    south_c[...] = jnp.maximum(lat, 0.0)
    north_c[...] = jnp.maximum(-lat, 0.0)
    own_c[...] = jnp.abs(lon) + jnp.abs(lat)


def first_body(
    even_ref, far_ref, near_ref, far_fields_ref, near_fields_ref, fields_ref, steps_ref, seen_ref, total_ref, cells_ref,
    gram_ref, south_ref, north_ref, full_ref, low_ref, high_ref, buf_ref, sum_ref, obs_ref, *scratch
):
    even = even_ref[0] == 1
    near, far = near_ref[...], far_ref[...]
    low_ref[...] = jnp.where(even, far, near)
    high_ref[...] = jnp.where(even, near, far)
    coefs, rest = scratch[:5], scratch[5:]
    near, far = near_fields_ref[...], far_fields_ref[...]
    full_ref[:, 0:HALO] = jnp.where(even, far, near)
    full_ref[:, HALO : HALO + CY] = fields_ref[...]
    full_ref[:, HALO + CY : ROWS] = jnp.where(even, near, far)
    fill_coefs(full_ref[1], full_ref[2], coefs)
    sum_ref[0:HALO] = jnp.zeros((HALO, LANES), jnp.float32)
    sum_ref[HALO : CY - HALO] = total_ref[...]
    sum_ref[CY - HALO : CY] = jnp.zeros((HALO, LANES), jnp.float32)
    use = observer(sum_ref, obs_ref)
    base = full_ref[0]

    for ref, out_ref in ((low_ref, south_ref), (high_ref, north_ref)):
        for u in range(PAIRS // 4):
            for i, rows in enumerate(unpacked(ref, 12 * u, 12 * (u + PAIRS // 4))):
                out_ref[4 * u + i] = rows
    edge_transport(base, south_ref, north_ref, coefs, steps_ref, buf_ref, use)

    def rows_of(p):
        return [obs_ref[p, 0:8], seen_ref[p, 0:8], seen_ref[p, 8:16], obs_ref[p, 24:32]]

    normal_terms(rows_of, sum_ref[...], cells_ref, gram_ref, *rest)


def solve(packed, weights):
    shape = (MEMBERS, LANES)
    wide = lane_of(shape)
    sub = lax.broadcasted_iota(jnp.int32, shape, 0)
    left = MEMBERS - 1.0
    low, high = packed[0], packed[1]
    packed = jnp.concatenate([low[0:8], high[0:8]], axis=0)
    ends = jnp.broadcast_to(low[8:9], shape)
    square = jnp.concatenate([packed, pltpu.roll(packed, 64, axis=1)], axis=0)
    padded = jnp.concatenate([square, jnp.zeros((LANES - PAIRS, LANES), jnp.float32)], axis=0)
    turned = jnp.transpose(padded)
    lane, row = wide[0:PAIRS], sub[0:PAIRS]
    top = jnp.where(lane >= row, pltpu.roll(square, LANES - 32, axis=1), turned[32:64])
    top = jnp.where(lane < 32, top, pltpu.roll(square, 32, axis=1))
    bottom = jnp.where(lane - 32 < row, square, pltpu.roll(turned[32:64], 32, axis=1))
    bottom = jnp.where(lane - 32 == row, pltpu.roll(ends, LANES - 32, axis=1)[0:PAIRS], bottom)
    bottom = jnp.where(lane < 32, turned[0:32], bottom)
    sums = jnp.concatenate([top, bottom], axis=0)
    project = jnp.sum(jnp.where(wide == sub, ends, 0.0), axis=1, keepdims=True)
    gradient = left * weights - jnp.broadcast_to(project, shape)
    lane = wide
    matrix = jnp.where(
        lane < MEMBERS,
        sums + jnp.where(lane == sub, left, 0.0),
        jnp.where(lane == MEMBERS, gradient, 0.0),
    )
    width = 8
    for start in range(0, MEMBERS, width):
        columns = [
            jnp.broadcast_to(matrix[:, start + j : start + j + 1], shape) for j in range(width)
        ]
        for j in range(width):
            k = start + j
            factor = jnp.where(sub == k, 0.0, columns[j] * (1.0 / columns[j][k : k + 1]))
            for later in range(j + 1, width):
                columns[later] = columns[later] - factor * columns[later][k : k + 1]
            matrix = matrix - factor * matrix[k : k + 1]
    diagonal = jnp.sum(jnp.where(lane == sub, matrix, 0.0), axis=1, keepdims=True)
    solved = matrix[:, MEMBERS : MEMBERS + 1] / diagonal
    return weights - jnp.broadcast_to(solved, shape)


def by_pair(weights):
    lane = lane_of((PAIRS, LANES))
    return jnp.where(lane < 64, weights[0:PAIRS], weights[PAIRS:MEMBERS])


def mix(pair_ref, anoms_ref):
    total = jnp.zeros(anoms_ref.shape[1:], jnp.float32)
    for p in range(PAIRS):
        total = total + pair_ref[p : p + 1] * anoms_ref[p]
    return total + pltpu.roll(total, 64, axis=1)


def second_body(
    sums_ref, south_ref, mid_ref, north_ref, full_ref, cells_ref,
    gram_ref, weights_ref, pair_ref, buf_ref, sum_ref, obs_ref, *scratch
):
    coefs, rest = scratch[:5], scratch[5:]
    fill_coefs(full_ref[1], full_ref[2], coefs)
    weights = solve(sums_ref[...], jnp.zeros((MEMBERS, LANES), jnp.float32))
    weights_ref[...] = weights
    pair_ref[...] = by_pair(weights)
    anoms = (south_ref, mid_ref, north_ref)
    base = full_ref[0] + jnp.concatenate([mix(pair_ref, ref) for ref in anoms], axis=0)
    edge = jnp.zeros((2, GROUP, HALO, LANES), jnp.float32)
    buf_ref[:, :, 0:HALO] = edge
    buf_ref[:, :, HALO + ROWS :] = edge
    sum_ref[...] = jnp.zeros((CY, LANES), jnp.float32)
    use = observer(sum_ref, obs_ref)
    for_groups(lambda first: transport(base, anoms, coefs, buf_ref, first, use))
    normal_terms(
        lambda p: blocks(obs_ref[p]), sum_ref[...], cells_ref, gram_ref, *rest
    )


def last_body(sums_ref, weights_ref, mid_ref, out_ref, pair_ref):
    weights = solve(sums_ref[...], weights_ref[...])
    pair_ref[...] = by_pair(weights)
    out_ref[...] = inner(blocks(mix(pair_ref, mid_ref)), 0)


def spread_body(pieces_ref, out_ref):
    lane = lane_of((8, LANES))
    for lev in range(LEV):
        for b in range(8):
            pieces = [pieces_ref[k % 2, 16 * lev + 2 * b + k // 2] for k in range(4)]
            for q in range(4):
                out = None
                for k in range(4):
                    moved = pltpu.roll(pieces[k], (32 * (k - q)) % LANES, axis=1)
                    out = moved if out is None else jnp.where(lane >= 32 * k, moved, out)
                out_ref[lev, 8 * q : 8 * q + 8, LANES * b : LANES * b + LANES] = out


def exchange(array, axes):
    return lax.all_to_all(array, axes, 0, 0, tiled=True)


def to_all(array, axes, count):
    return exchange(jnp.broadcast_to(array[None], (count, *array.shape)), axes)


def both_cores(array):
    return lax.all_gather(array, "core")


def sum_everywhere(packed):
    shape = (5, 2, LANES)
    halves = jnp.broadcast_to(packed.reshape(1, 2, 1, *shape), (2, 2, 8, *shape))
    part = jnp.sum(exchange(halves.reshape(32, *shape), PLANE), axis=0)
    part = jnp.sum(to_all(part, "z", 16), axis=0).reshape(10, LANES)
    return both_cores(part)


def local(
    background, anomalies, courant_lon, courant_lat, obs_value, obs_weight, obs_column, obs_level
):
    chunk = lax.axis_index(MEM).astype(jnp.int32).reshape(1)
    pieces = call(pack_body, f32(MEMBERS * 12, LANES), in_specs=[VMEM])(anomalies[0])
    pieces = exchange(pieces.reshape(MEMBERS, 3, 4, LANES), MEM).reshape(MEMBERS * 12, LANES)
    nobs = obs_value.shape[0]
    flat = [a.reshape(1, nobs) for a in (obs_value, obs_weight, obs_column, obs_level)]
    cells = call(cells_body, f32(2, CY, LANES), in_specs=[SMEM] + [VMEM] * 4)(chunk, *flat)
    even = (1 - lax.axis_index("x") % 2).astype(jnp.int32).reshape(1)
    to_far = [(t, t + 1 if t % 2 else t - 1) for t in range(1, 7)]
    to_near = [(t, t - 1 if t % 2 else t + 1) for t in range(8)]
    fields, near_fields, far_fields = call(
        fields_body,
        (f32(3, CY, LANES), f32(3, HALO, LANES), f32(3, HALO, LANES)),
        in_specs=[SMEM] * 2 + [VMEM] * 3,
    )(chunk, even, background, courant_lon, courant_lat)
    far_fields = lax.ppermute(far_fields, TILE, to_far)
    near_fields = lax.ppermute(near_fields, TILE, to_near)
    pieces, fields, cells, far_fields, near_fields = lax.optimization_barrier(
        (pieces, fields, cells, far_fields, near_fields)
    )
    near_edge, far_edge = call(
        edges_body, (f32(EDGE, LANES), f32(EDGE, LANES)), in_specs=[SMEM, VMEM]
    )(even, pieces)
    far = lax.ppermute(far_edge, TILE, to_far)
    near = lax.ppermute(near_edge, TILE, to_near)
    mid, steps, seen, total = call(
        inside_body,
        (
            f32(PAIRS, CY, LANES),
            f32(NSTEP, PAIRS, ROWS, LANES),
            f32(PAIRS, CY - 2 * HALO, LANES),
            f32(CY - 2 * HALO, LANES),
        ),
        [pltpu.VMEM((CY, LANES), jnp.float32)] * 5,
        in_specs=[VMEM] * 2,
    )(pieces, fields)
    rest = [
        pltpu.VMEM((CY, LANES), jnp.float32),
        pltpu.VMEM((PAIRS, CY, LANES), jnp.float32),
        *[pltpu.VMEM((ROWS, LANES), jnp.float32)] * 5,
        pltpu.VMEM((MEMBERS * 8, LANES), jnp.float32),
        pltpu.VMEM((MEMBERS, 8 * LANES), jnp.float32),
        pltpu.VMEM((LANES, 8 * LANES), jnp.float32),
    ]
    pair = pltpu.VMEM((PAIRS, LANES), jnp.float32)
    gram, south, north, full = call(
        first_body,
        (f32(PACKED, LANES), *[f32(PAIRS, HALO, LANES)] * 2, f32(3, ROWS, LANES)),
        [
            *[pltpu.VMEM((EDGE, LANES), jnp.float32)] * 2,
            pltpu.VMEM((2, PAIRS, 3 * HALO, LANES), jnp.float32),
            *rest,
        ],
        in_specs=[SMEM] + [VMEM] * 9,
    )(even, far, near, far_fields, near_fields, fields, steps, seen, total, cells)
    gram, weights = call(
        second_body,
        (f32(PACKED, LANES), f32(MEMBERS, LANES)),
        [pair, pltpu.VMEM((2, GROUP, ROWS + 2 * HALO, LANES), jnp.float32), *rest],
        in_specs=[VMEM] * 6,
    )(sum_everywhere(gram), south, mid, north, full, cells)
    part = call(last_body, f32(8, LANES), [pair], in_specs=[VMEM] * 3)(
        sum_everywhere(gram), weights, mid
    )
    parts = both_cores(to_all(part, ("z", "yl"), 32))
    return call(spread_body, f32(LEV, CY, NX), in_specs=[VMEM])(parts)


def solution(mesh):
    fine = Mesh(mesh.devices.reshape(16, 2, 2, 2, 4), ("z", "yl", "core", "yh", "x"))
    return jax.shard_map(
        local,
        mesh=fine,
        in_specs=(
            P(None, TILE, None),
            P(MEM, None, TILE, None),
            P(None, TILE, None),
            P(None, TILE, None),
            P(TILE),
            P(TILE),
            P(TILE),
            P(TILE),
        ),
        out_specs=P(None, TILE, None),
        check_vma=False,
    )
```

```python
import functools

import jax
import jax.numpy as jnp
from jax import lax
from jax.experimental import pallas as pl
from jax.experimental.pallas import tpu as pltpu
from jax.sharding import Mesh, PartitionSpec as P

NSTEP = 8
MEMBERS = 64
PAIRS = 32
GROUP = 16
LEV = 2
CY = 32
NX = 1024
CHUNK = 32
HALO = 8
ROWS = CY + 2 * HALO
EDGE = 12 * MEMBERS // 4
LANES = 128
PACKED = 20
WHOLE = 24

MEM = ("z", "yl", "core")
TILE = ("yh", "x")
PLANE = ("yl", "core", "yh", "x")
VMEM = pl.BlockSpec(memory_space=pltpu.VMEM)
SMEM = pl.BlockSpec(memory_space=pltpu.SMEM)


def lane_of(shape):
    return lax.broadcasted_iota(jnp.int32, shape, len(shape) - 1)


def call(body, out, scratch=(), in_specs=None, vmem=40 << 20):
    return pl.pallas_call(
        body,
        out_shape=out,
        in_specs=in_specs,
        out_specs=jax.tree.map(lambda _: VMEM, out),
        scratch_shapes=list(scratch),
        compiler_params=pltpu.CompilerParams(vmem_limit_bytes=vmem),
    )


def f32(*shape):
    return jax.ShapeDtypeStruct(shape, jnp.float32)


def pack_body(own_ref, pieces_ref):
    lane = lane_of((8, LANES))
    for lev in range(LEV):
        turned = []
        for q in range(4):
            rolled = [
                pltpu.roll(own_ref[lev, 8 * q : 8 * q + 8, LANES * b : LANES * b + LANES], HALO, axis=1)
                for b in range(8)
            ]
            shifted = [jnp.where(lane < HALO, rolled[b - 1], rolled[b]) for b in range(8)]
            turned.append(
                [
                    [pltpu.roll(block, 32 * n, axis=1) if n else block for n in range(4)]
                    for block in shifted
                ]
            )

        for b in range(8):
            for k in range(4):
                at = 12 * (32 * lev + 4 * b + k)
                near = [turned[q][b][(q - k) % 4] for q in range(4)]
                after = near if k < 3 else [turned[q][(b + 1) % 8][(q - k) % 4] for q in range(4)]
                pieces_ref[at + 4 : at + 12] = in_groups(near)
                rest = in_groups(after[3:] + after[:3])
                other = pltpu.roll(rest, 16, axis=1)
                pieces_ref[at : at + 4] = jnp.where(lane[0:4] % 32 < 16, rest[0:4], other[4:8])


def in_groups(parts):
    group = lane_of(parts[0].shape) // 32
    out = parts[0]
    for q in range(1, 4):
        out = jnp.where(group == q, parts[q], out)
    return out


def fields_body(chunk_ref, even_ref, bg_ref, lon_ref, lat_ref, fields_ref, near_ref, far_ref):
    chunk, even = chunk_ref[0], even_ref[0] == 1
    lev, b, k = chunk // 32, chunk % 32 // 4, chunk % 4
    wide = lane_of((CY, LANES))

    def block(ref, index):
        return ref[lev, :, pl.ds(pl.multiple_of(index * LANES, LANES), LANES)]

    for index, ref in enumerate((bg_ref, lon_ref, lat_ref)):
        mid = block(ref, b)
        mid = jnp.where((wide >= LANES - HALO) & (k == 0), block(ref, (b + 7) % 8), mid)
        mid = jnp.where((wide < HALO) & (k == 3), block(ref, (b + 1) % 8), mid)
        mid = pltpu.roll(mid, (HALO - CHUNK * k + LANES) % LANES, axis=1)
        mid = jnp.where(wide < CHUNK + 2 * HALO, mid, 0.0)
        mid = jnp.where(wide < 64, mid, pltpu.roll(mid, 64, axis=1))
        fields_ref[index] = mid
        near_ref[index] = jnp.where(even, mid[CY - HALO :], mid[:HALO])
        far_ref[index] = jnp.where(even, mid[:HALO], mid[CY - HALO :])


def edges_body(even_ref, x_ref, near_ref, far_ref):
    even = even_ref[0] == 1

    def put(at, count, low, high):
        near_ref[at : at + count] = jnp.where(even, high, low)
        far_ref[at : at + count] = jnp.where(even, low, high)

    for u in range(MEMBERS // 4):
        for row, count in ((0, 4), (4, 8)):
            lows, highs = [], []
            for i in range(4):
                at = 12 * (4 * u + i) + row
                piece = x_ref[at : at + count]
                lows.append(pltpu.roll(piece, 32 * i, axis=1) if i else piece)
                highs.append(pltpu.roll(piece, 32 * i + 32, axis=1) if i < 3 else piece)
            if row == 0:
                lows, highs = lows[3:] + lows[:3], highs[3:] + highs[:3]
            put(12 * u + row, count, in_groups(lows), in_groups(highs))


def unpacked(ref, first, second):
    lane = lane_of((8, LANES))
    place = lane % 64
    mains, rests = [], []
    for at, turn in ((first, 0), (second, 64)):
        rest = ref[pl.ds(at, 4)]
        rest = jnp.concatenate([rest, pltpu.roll(rest, LANES - 16, axis=1)], axis=0)
        main = ref[pl.ds(at + 4, 8)]
        mains.append(pltpu.roll(main, turn, axis=1) if turn else main)
        rests.append(pltpu.roll(rest, turn, axis=1) if turn else rest)
    sources = [mains[0], rests[0], mains[1], rests[1]]
    out = []
    for q in range(4):
        whole = in_groups([sources[(group - q) % 4] for group in range(4)])
        whole = pltpu.roll(whole, LANES - 32 * q, axis=1) if q else whole
        out.append(jnp.where(place < CHUNK + 2 * HALO, whole, 0.0))
    return out


def advance(state, south, north, coefs, at):
    west_c, east_c, south_c, north_c, own_c = (ref[at : at + 8] for ref in coefs)
    west = pltpu.roll(state, 1, axis=1)
    east = pltpu.roll(state, LANES - 1, axis=1)
    speed = 0.85 + 0.15 * jnp.tanh(state)
    change = west_c * west + east_c * east
    change = change + (south_c * south + north_c * north)
    return state + speed * (change - own_c * state)


def inside_body(x_ref, fields_ref, mid_ref, steps_ref, seen_ref, total_ref, *coefs):
    fill_coefs(fields_ref[1], fields_ref[2], coefs)
    total_ref[...] = jnp.zeros((CY - 2 * HALO, LANES), jnp.float32)

    edge = jnp.zeros((HALO, LANES), jnp.float32)

    def one(index, carry):
        pairs = [index * GROUP + p for p in range(GROUP)]
        for p in pairs:
            for step in range(NSTEP):
                steps_ref[step, p, 0:HALO] = edge
                steps_ref[step, p, HALO + CY : ROWS] = edge
            for q, out in enumerate(unpacked(x_ref, 12 * p, 12 * (p + PAIRS))):
                rows = slice(8 * q, 8 * q + 8)
                mid_ref[p, rows] = out
                steps_ref[0, p, HALO + 8 * q : HALO + 8 * q + 8] = fields_ref[0, rows] + 0.5 * out
        for step in range(NSTEP):
            for q in range(4) if step < NSTEP - 1 else (1, 2):
                at = 8 * q
                for p in pairs:
                    now = steps_ref.at[step, p]
                    put = HALO + at
                    state = advance(
                        now[put : put + 8], now[put - 1 : put + 7], now[put + 1 : put + 9], coefs, at
                    )
                    if step < NSTEP - 1:
                        steps_ref[step + 1, p, put : put + 8] = state
                    else:
                        seen = state + 0.25 * state * state
                        seen_ref[p, at - 8 : at] = seen
                        total_ref[at - 8 : at] += seen
        return carry

    lax.fori_loop(0, PAIRS // GROUP, one, 0)


def cells_body(chunk_ref, value_ref, weight_ref, column_ref, level_ref, out_ref):
    chunk = chunk_ref[0]
    column = column_ref[...]
    row = column // NX
    offset = column % NX - CHUNK * (chunk % 32)
    inside = (offset >= 0) & (offset < CHUNK) & (level_ref[...] == chunk // 32)
    lane = jnp.where(inside, HALO + offset, -1)
    square = weight_ref[...] * weight_ref[...]
    nobs = column.shape[1]
    at_row = lax.broadcasted_iota(jnp.int32, (CY, nobs), 0) == row
    at_lane = (lax.broadcasted_iota(jnp.int32, (LANES, nobs), 0) == lane).astype(jnp.bfloat16)
    parts = []
    for value in (square, square * value_ref[...]):
        left = jnp.where(at_row, value, 0.0)
        for _ in range(3):
            part = left.astype(jnp.bfloat16)
            parts.append(part)
            left = left - part.astype(jnp.float32)
    sums = lax.dot_general(
        jnp.concatenate(parts, axis=0),
        at_lane,
        (((1,), (1,)), ((), ())),
        preferred_element_type=jnp.float32,
    )
    for index in range(2):
        base = 3 * CY * index
        total = sums[base : base + CY] + sums[base + CY : base + 2 * CY]
        total = total + sums[base + 2 * CY : base + 3 * CY]
        out_ref[index] = total


def transport(base, anoms, coefs, buf_ref, first, use):
    for p in range(GROUP):
        at = HALO
        for ref in anoms:
            rows = ref.shape[1]
            buf_ref[0, p, at : at + rows] = base[at - HALO : at - HALO + rows] + 0.5 * ref[first + p]
            at += rows
    for step in range(NSTEP):
        for low in range(0, ROWS, 8) if step < NSTEP - 1 else range(HALO, HALO + CY, 8):
            at = HALO + low
            for p in range(GROUP):
                now = buf_ref.at[step % 2, p]
                state = advance(
                    now[at : at + 8], now[at - 1 : at + 7], now[at + 1 : at + 9], coefs, low
                )
                if step < NSTEP - 1:
                    buf_ref[(step + 1) % 2, p, at : at + 8] = state
                else:
                    use(first + p, low - HALO, state)


def edge_transport(base, low_ref, high_ref, coefs, steps_ref, buf_ref, use):
    for p in range(PAIRS):
        buf_ref[0, p, 0:HALO] = base[0:HALO] + 0.5 * low_ref[p]
        buf_ref[1, p, 2 * HALO : 3 * HALO] = base[HALO + CY :] + 0.5 * high_ref[p]
    for step in range(NSTEP):
        for edge in range(2):
            inside, put, at, low = (
                (HALO + step, step + 8, step + 1, step + 1)
                if edge == 0
                else (CY - step, 8 - step, 15 - step, 39 - step)
            )
            for p in range(PAIRS):
                now = buf_ref.at[edge, p]
                now[put : put + 8] = steps_ref[step, p, inside : inside + 8]
                state = advance(
                    now[at : at + 8], now[at - 1 : at + 7], now[at + 1 : at + 9], coefs, low
                )
                if step < NSTEP - 1:
                    now[at : at + 8] = state
                else:
                    use(p, (CY - HALO) * edge, state)


def blocks(rows):
    return [rows[8 * q : 8 * q + 8] for q in range(4)]


def inner(rows, start):
    lane = lane_of((8, LANES))
    out = None
    for q in range(4):
        moved = pltpu.roll(rows[q], (32 * q - HALO - start) % LANES, axis=1)
        out = moved if out is None else jnp.where(lane >= 32 * q, moved, out)
    return out


def observer(total_ref, obs_ref):
    def use(p, row, state):
        seen = state + 0.25 * state * state
        obs_ref[p, row : row + 8] = seen
        total_ref[row : row + 8] += seen

    return use


def for_groups(work):
    def one(index, carry):
        work(index * GROUP)
        return carry

    lax.fori_loop(0, PAIRS // GROUP, one, 0)


def split(value):
    high = value.astype(jnp.bfloat16)
    return high, (value - high.astype(jnp.float32)).astype(jnp.bfloat16)


def by_rows(left, right):
    return lax.dot_general(
        left, right, (((1,), (1,)), ((), ())), preferred_element_type=jnp.float32
    )


def normal_terms(rows_of, total, cells_ref, gram_ref, dev_ref, left_ref, right_ref):
    center = (total + pltpu.roll(total, 64, axis=1)) * (1.0 / MEMBERS)
    for p in range(PAIRS):
        dev = [rows - center[8 * q : 8 * q + 8] for q, rows in enumerate(rows_of(p))]
        for half in range(2):
            at = 8 * (p + PAIRS * half)
            dev_ref[at : at + 8] = inner(dev, 64 * half)
    weight, weighted = cells_ref[0], cells_ref[1]
    aim = inner(blocks(2.0 * (weighted - weight * center)), 0)
    weight = inner(blocks(4.0 * weight), 0)
    right_ref[MEMBERS:LANES, :] = jnp.zeros((LANES - MEMBERS, 8 * LANES), jnp.float32)
    for r in range(8):
        rows = dev_ref[pl.ds(r, MEMBERS, stride=8), :]
        left_ref[:, LANES * r : LANES * r + LANES] = rows
        right_ref[0:MEMBERS, LANES * r : LANES * r + LANES] = rows * weight[r : r + 1]
        right_ref[MEMBERS : MEMBERS + 1, LANES * r : LANES * r + LANES] = aim[r : r + 1]
    (left_high, left_low), (right_high, right_low) = split(left_ref[...]), split(right_ref[...])
    gram = by_rows(left_high, right_high)
    gram = gram + (by_rows(left_high, right_low) + by_rows(left_low, right_high))
    wide = lane_of((MEMBERS, LANES))
    sub = lax.broadcasted_iota(jnp.int32, (MEMBERS, LANES), 0)
    column = jnp.broadcast_to(gram[:, MEMBERS : MEMBERS + 1], (MEMBERS, LANES))
    project = jnp.sum(jnp.where(wide == sub, column, 0.0), axis=0, keepdims=True)
    top, bottom = gram[0:PAIRS], gram[PAIRS:MEMBERS]
    lane, sub = wide[0:PAIRS], sub[0:PAIRS]
    diagonal = jnp.sum(jnp.where(lane - 32 == sub, bottom, 0.0), axis=0, keepdims=True)
    square = jnp.where(lane - 32 >= sub, pltpu.roll(top, 32, axis=1), bottom)
    square = jnp.where(lane < 32, pltpu.roll(top, LANES - 32, axis=1), square)
    packed = jnp.where(lane[0:16] < 64, square[0:16], pltpu.roll(square[16:32], 64, axis=1))
    gram_ref[...] = jnp.zeros((WHOLE, LANES), jnp.float32)
    gram_ref[0:8] = packed[0:8]
    gram_ref[8:9] = jnp.where(lane[0:1] < 64, project, pltpu.roll(diagonal, 32, axis=1))
    gram_ref[10:18] = packed[8:16]


def fill_coefs(lon, lat, coefs):
    west_c, east_c, south_c, north_c, own_c = coefs
    west_c[...] = jnp.maximum(lon, 0.0)
    east_c[...] = jnp.maximum(-lon, 0.0)
    south_c[...] = jnp.maximum(lat, 0.0)
    north_c[...] = jnp.maximum(-lat, 0.0)
    own_c[...] = jnp.abs(lon) + jnp.abs(lat)


def first_body(
    even_ref, far_ref, near_ref, far_fields_ref, near_fields_ref, fields_ref, steps_ref, seen_ref, total_ref, cells_ref,
    gram_ref, south_ref, north_ref, full_ref, low_ref, high_ref, buf_ref, sum_ref, obs_ref, *scratch
):
    even = even_ref[0] == 1
    near, far = near_ref[...], far_ref[...]
    low_ref[...] = jnp.where(even, far, near)
    high_ref[...] = jnp.where(even, near, far)
    coefs, rest = scratch[:5], scratch[5:]
    near, far = near_fields_ref[...], far_fields_ref[...]
    full_ref[:, 0:HALO] = jnp.where(even, far, near)
    full_ref[:, HALO : HALO + CY] = fields_ref[...]
    full_ref[:, HALO + CY : ROWS] = jnp.where(even, near, far)
    fill_coefs(full_ref[1], full_ref[2], coefs)
    sum_ref[0:HALO] = jnp.zeros((HALO, LANES), jnp.float32)
    sum_ref[HALO : CY - HALO] = total_ref[...]
    sum_ref[CY - HALO : CY] = jnp.zeros((HALO, LANES), jnp.float32)
    use = observer(sum_ref, obs_ref)
    base = full_ref[0]

    for ref, out_ref in ((low_ref, south_ref), (high_ref, north_ref)):
        for u in range(PAIRS // 4):
            for i, rows in enumerate(unpacked(ref, 12 * u, 12 * (u + PAIRS // 4))):
                out_ref[4 * u + i] = rows
    edge_transport(base, south_ref, north_ref, coefs, steps_ref, buf_ref, use)

    def rows_of(p):
        return [obs_ref[p, 0:8], seen_ref[p, 0:8], seen_ref[p, 8:16], obs_ref[p, 24:32]]

    normal_terms(rows_of, sum_ref[...], cells_ref, gram_ref, *rest)


def solve(packed, weights):
    shape = (MEMBERS, LANES)
    wide = lane_of(shape)
    sub = lax.broadcasted_iota(jnp.int32, shape, 0)
    left = MEMBERS - 1.0
    low, high = packed[0], packed[1]
    packed = jnp.concatenate([low[0:8], high[0:8]], axis=0)
    ends = jnp.broadcast_to(low[8:9], shape)
    square = jnp.concatenate([packed, pltpu.roll(packed, 64, axis=1)], axis=0)
    padded = jnp.concatenate([square, jnp.zeros((LANES - PAIRS, LANES), jnp.float32)], axis=0)
    turned = jnp.transpose(padded)
    lane, row = wide[0:PAIRS], sub[0:PAIRS]
    top = jnp.where(lane >= row, pltpu.roll(square, LANES - 32, axis=1), turned[32:64])
    top = jnp.where(lane < 32, top, pltpu.roll(square, 32, axis=1))
    bottom = jnp.where(lane - 32 < row, square, pltpu.roll(turned[32:64], 32, axis=1))
    bottom = jnp.where(lane - 32 == row, pltpu.roll(ends, LANES - 32, axis=1)[0:PAIRS], bottom)
    bottom = jnp.where(lane < 32, turned[0:32], bottom)
    sums = jnp.concatenate([top, bottom], axis=0)
    project = jnp.sum(jnp.where(wide == sub, ends, 0.0), axis=1, keepdims=True)
    gradient = left * weights - jnp.broadcast_to(project, shape)
    lane = wide
    matrix = jnp.where(
        lane < MEMBERS,
        sums + jnp.where(lane == sub, left, 0.0),
        jnp.where(lane == MEMBERS, gradient, 0.0),
    )
    width = 8
    for start in range(0, MEMBERS, width):
        columns = [
            jnp.broadcast_to(matrix[:, start + j : start + j + 1], shape) for j in range(width)
        ]
        for j in range(width):
            k = start + j
            factor = jnp.where(sub == k, 0.0, columns[j] * (1.0 / columns[j][k : k + 1]))
            for later in range(j + 1, width):
                columns[later] = columns[later] - factor * columns[later][k : k + 1]
            matrix = matrix - factor * matrix[k : k + 1]
    diagonal = jnp.sum(jnp.where(lane == sub, matrix, 0.0), axis=1, keepdims=True)
    solved = matrix[:, MEMBERS : MEMBERS + 1] / diagonal
    return weights - jnp.broadcast_to(solved, shape)


def by_pair(weights):
    lane = lane_of((PAIRS, LANES))
    return jnp.where(lane < 64, weights[0:PAIRS], weights[PAIRS:MEMBERS])


def mix(pair_ref, anoms_ref):
    total = jnp.zeros(anoms_ref.shape[1:], jnp.float32)
    weights = pair_ref[...]
    for p in range(PAIRS):
        total = total + weights[p : p + 1] * anoms_ref[p]
    return total + pltpu.roll(total, 64, axis=1)


def second_body(
    sums_ref, south_ref, mid_ref, north_ref, full_ref, cells_ref,
    gram_ref, weights_ref, pair_ref, buf_ref, sum_ref, obs_ref, *scratch
):
    coefs, rest = scratch[:5], scratch[5:]
    fill_coefs(full_ref[1], full_ref[2], coefs)
    weights = solve(sums_ref[...], jnp.zeros((MEMBERS, LANES), jnp.float32))
    weights_ref[...] = weights
    pair_ref[...] = by_pair(weights)
    anoms = (south_ref, mid_ref, north_ref)
    base = full_ref[0] + jnp.concatenate([mix(pair_ref, ref) for ref in anoms], axis=0)
    edge = jnp.zeros((2, GROUP, HALO, LANES), jnp.float32)
    buf_ref[:, :, 0:HALO] = edge
    buf_ref[:, :, HALO + ROWS :] = edge
    sum_ref[...] = jnp.zeros((CY, LANES), jnp.float32)
    use = observer(sum_ref, obs_ref)
    for_groups(lambda first: transport(base, anoms, coefs, buf_ref, first, use))
    normal_terms(
        lambda p: blocks(obs_ref[p]), sum_ref[...], cells_ref, gram_ref, *rest
    )


def last_body(sums_ref, weights_ref, mid_ref, out_ref, pair_ref):
    weights = solve(sums_ref[...], weights_ref[...])
    pair_ref[...] = by_pair(weights)
    out_ref[...] = inner(blocks(mix(pair_ref, mid_ref)), 0)


def spread_body(pieces_ref, out_ref):
    lane = lane_of((8, LANES))
    for lev in range(LEV):
        for b in range(8):
            pieces = [pieces_ref[k % 2, 16 * lev + 2 * b + k // 2] for k in range(4)]
            for q in range(4):
                out = None
                for k in range(4):
                    moved = pltpu.roll(pieces[k], (32 * (k - q)) % LANES, axis=1)
                    out = moved if out is None else jnp.where(lane >= 32 * k, moved, out)
                out_ref[lev, 8 * q : 8 * q + 8, LANES * b : LANES * b + LANES] = out


def exchange(array, axes):
    return lax.all_to_all(array, axes, 0, 0, tiled=True)


def to_all(array, axes, count):
    return exchange(jnp.broadcast_to(array[None], (count, *array.shape)), axes)


def both_cores(array):
    return lax.all_gather(array, "core")


def sum_everywhere(packed):
    shape = (5, 2, LANES)
    halves = jnp.broadcast_to(packed[:PACKED].reshape(1, 2, 1, *shape), (2, 2, 8, *shape))
    part = jnp.sum(exchange(halves.reshape(32, *shape), PLANE), axis=0)
    part = jnp.sum(to_all(part, "z", 16), axis=0).reshape(10, LANES)
    return both_cores(jnp.pad(part, ((0, 6), (0, 0))))


def local(
    background, anomalies, courant_lon, courant_lat, obs_value, obs_weight, obs_column, obs_level
):
    chunk = lax.axis_index(MEM).astype(jnp.int32).reshape(1)
    pieces = call(pack_body, f32(MEMBERS * 12, LANES), in_specs=[VMEM])(anomalies[0])
    pieces = exchange(pieces.reshape(MEMBERS, 3, 4, LANES), MEM).reshape(MEMBERS * 12, LANES)
    nobs = obs_value.shape[0]
    flat = [a.reshape(1, nobs) for a in (obs_value, obs_weight, obs_column, obs_level)]
    cells = call(cells_body, f32(2, CY, LANES), in_specs=[SMEM] + [VMEM] * 4)(chunk, *flat)
    even = (1 - lax.axis_index("x") % 2).astype(jnp.int32).reshape(1)
    to_far = [(t, t + 1 if t % 2 else t - 1) for t in range(1, 7)]
    to_near = [(t, t - 1 if t % 2 else t + 1) for t in range(8)]
    fields, near_fields, far_fields = call(
        fields_body,
        (f32(3, CY, LANES), f32(3, HALO, LANES), f32(3, HALO, LANES)),
        in_specs=[SMEM] * 2 + [VMEM] * 3,
    )(chunk, even, background, courant_lon, courant_lat)
    far_fields = lax.ppermute(far_fields, TILE, to_far)
    near_fields = lax.ppermute(near_fields, TILE, to_near)
    pieces, fields, cells, far_fields, near_fields = lax.optimization_barrier(
        (pieces, fields, cells, far_fields, near_fields)
    )
    near_edge, far_edge = call(
        edges_body, (f32(EDGE, LANES), f32(EDGE, LANES)), in_specs=[SMEM, VMEM]
    )(even, pieces)
    far = lax.ppermute(far_edge, TILE, to_far)
    near = lax.ppermute(near_edge, TILE, to_near)
    mid, steps, seen, total = call(
        inside_body,
        (
            f32(PAIRS, CY, LANES),
            f32(NSTEP, PAIRS, ROWS, LANES),
            f32(PAIRS, CY - 2 * HALO, LANES),
            f32(CY - 2 * HALO, LANES),
        ),
        [pltpu.VMEM((CY, LANES), jnp.float32)] * 5,
        in_specs=[VMEM] * 2,
    )(pieces, fields)
    rest = [
        pltpu.VMEM((CY, LANES), jnp.float32),
        pltpu.VMEM((PAIRS, CY, LANES), jnp.float32),
        *[pltpu.VMEM((ROWS, LANES), jnp.float32)] * 5,
        pltpu.VMEM((MEMBERS * 8, LANES), jnp.float32),
        pltpu.VMEM((MEMBERS, 8 * LANES), jnp.float32),
        pltpu.VMEM((LANES, 8 * LANES), jnp.float32),
    ]
    pair = pltpu.VMEM((PAIRS, LANES), jnp.float32)
    gram, south, north, full = call(
        first_body,
        (f32(WHOLE, LANES), *[f32(PAIRS, HALO, LANES)] * 2, f32(3, ROWS, LANES)),
        [
            *[pltpu.VMEM((EDGE, LANES), jnp.float32)] * 2,
            pltpu.VMEM((2, PAIRS, 3 * HALO, LANES), jnp.float32),
            *rest,
        ],
        in_specs=[SMEM] + [VMEM] * 9,
    )(even, far, near, far_fields, near_fields, fields, steps, seen, total, cells)
    gram, weights = call(
        second_body,
        (f32(WHOLE, LANES), f32(MEMBERS, LANES)),
        [pair, pltpu.VMEM((2, GROUP, ROWS + 2 * HALO, LANES), jnp.float32), *rest],
        in_specs=[VMEM] * 6,
    )(sum_everywhere(gram), south, mid, north, full, cells)
    part = call(last_body, f32(8, LANES), [pair], in_specs=[VMEM] * 3)(
        sum_everywhere(gram), weights, mid
    )
    parts = both_cores(to_all(part, ("z", "yl"), 32))
    return call(spread_body, f32(LEV, CY, NX), in_specs=[VMEM])(parts)


def solution(mesh):
    fine = Mesh(mesh.devices.reshape(16, 2, 2, 2, 4), ("z", "yl", "core", "yh", "x"))
    return jax.shard_map(
        local,
        mesh=fine,
        in_specs=(
            P(None, TILE, None),
            P(MEM, None, TILE, None),
            P(None, TILE, None),
            P(None, TILE, None),
            P(TILE),
            P(TILE),
            P(TILE),
            P(TILE),
        ),
        out_specs=P(None, TILE, None),
        check_vma=False,
    )
```
